256 devices in a mesh: dp: 4 (over x), tiles: 64 (over z, y, core).
Axes of the slice: x: 4, y: 4, z: 8, core: 2. Of those that a mesh axis runs over, the one named last changes fastest.
Arguments:
- fields: bfloat16 [4, 256, 16, 3072], P('dp', 'tiles'), may hold values from -6 to 6
- ocean_mask: int32 [256, 16, 16], P('tiles'), may hold values 0 or 1
- neighbours: int32 [256, 8], P('tiles'), may hold values from -1 to 255, as said below
- dw_kernel: float32 [49, 192], replicated, may hold values from -0.875 to 0.875
- ln_gain: float32 [192], replicated, may hold values from 0.5 to 2
- ln_bias: float32 [192], replicated, may hold values from -3 to 3
- w_in: bfloat16 [192, 768], replicated, may hold values from -0.4375 to 0.4375
- b_in: float32 [768], replicated, may hold values from -3 to 3
- w_out: bfloat16 [768, 192], replicated, may hold values from -0.21875 to 0.21875
- layer_scale: float32 [192], replicated, may hold values from 0.3 to 1.5
- cotangent: bfloat16 [4, 256, 16, 3072], P('dp', 'tiles'), may hold values from -6 to 6
Outputs:
- block_out: bfloat16 [4, 256, 16, 3072], P('dp', 'tiles')
- field_grad: bfloat16 [4, 256, 16, 3072], P('dp', 'tiles')
- grad_kernel: float32 [49, 192], replicated
- grad_gain: float32 [192], replicated
- grad_shift: float32 [192], replicated
- grad_in: float32 [192, 768], replicated
- grad_bias: float32 [768], replicated
- grad_out: float32 [768, 192], replicated
- grad_scale: float32 [192], replicated
The draws below stay inside these ranges and needn't reach their ends.
Inputs may be any that keep to these rules, and one draw needn't show every extreme that they name: `neighbours`: row s lists the slots of the tiles around tile s in the order of the steps, -1 where that tile is land or off the slab; the relation is symmetric. Slots number the ocean tiles row by row, so the neighbour at (0,-1) holds slot s - 1, the one at (0,1) slot s + 1, those with dy = -1 lower and those with dy = 1 higher slots, all within 9 of s.
All inputs are finite; a program needn't handle non-finite values. No bound on the sum of `ocean_mask` on one device may be relied on, other than what follows from the above.
Results may differ from the reference program's by a relative error of at most 0.007.
Values may be sent and summed in bfloat16 or wider, within the bound.
No kernel may reach another device: no remote copies, remote signals or barrier semaphores. Data moves between devices by JAX's collectives and lax.ppermute only.
A program may use at most 64 MiB of HBM per device.

```python
import math
import jax
import jax.numpy as jnp
from jax import lax

C = 192
HID = 768
KS = 7
TILE = 16
TPD = 4
TGX = 8
SLOTS = 256
TGY = 40
BATCH = 4
CELLS = 262144
N_TILES = 64


DIRECTIONS = ((-1, -1), (-1, 0), (-1, 1), (0, -1), (0, 1), (1, -1), (1, 0), (1, 1))


def draw_neighbours(key, part):
    key = jax.random.fold_in(key, 7)
    grid_count = TGY * TGX
    position = jnp.arange(grid_count, dtype=jnp.int32)
    grid_row = position // TGX
    grid_col = position % TGX
    scores = jax.random.randint(key, (grid_count,), 0, 4096, dtype=jnp.int32)
    scores = jnp.where(grid_row < 2, -1, scores) * grid_count + position
    ordering = jnp.argsort(scores, stable=True)
    ranking = jnp.zeros((grid_count,), jnp.int32).at[ordering].set(position)
    ocean_tile = ranking < SLOTS
    slot_of = jnp.cumsum(ocean_tile.astype(jnp.int32)) - 1
    columns = []
    for delta_row, delta_col in DIRECTIONS:
        near_row = grid_row + delta_row
        near_col = grid_col + delta_col
        inside = (near_row >= 0) & (near_row < TGY) & (near_col >= 0) & (near_col < TGX)
        near_cell = jnp.clip(near_row, 0, TGY - 1) * TGX + jnp.clip(near_col, 0, TGX - 1)
        columns.append(jnp.where(inside & ocean_tile[near_cell], slot_of[near_cell], -1))
    near_table = jnp.stack(columns, axis=1)
    chosen = jnp.argsort(jnp.where(ocean_tile, position, position + grid_count), stable=True)[:SLOTS]
    return near_table[chosen].astype(jnp.int32)


def touch_ends(values, own_key, smallest, top_value):
    longest = values.shape.index(max(values.shape))
    spots = []
    for shift in (0, 1):
        where = [jax.random.randint(jax.random.fold_in(own_key, axis), (), 0, length) for axis, length in enumerate(values.shape)]
        where[longest] = (where[longest] + shift) % values.shape[longest]
        spots.append(tuple(where))
    return values.at[spots[0]].set(smallest).at[spots[1]].set(top_value)


def level_of(key, dims, shards, low, top_value):
    def one(dim, shards_of):
        steps = jax.random.uniform(jax.random.fold_in(jax.random.fold_in(key, 6), dim), (shards_of,), jnp.float32, low / len(shards), top_value / len(shards))
        return jnp.repeat(jnp.exp(steps), dims[dim] // shards_of).reshape((-1,) + (1,) * (len(dims) - dim - 1))

    loudness = one(*shards[0])
    for cut in shards[1:]:
        loudness = loudness * one(*cut)
    return loudness


def noise(rng, shape, spread, reach, split=(), held_as=jnp.bfloat16):
    gain = level_of(rng, shape, split, -0.22, 0.18) if split else 1.0
    drawn = jax.random.normal(rng, shape, jnp.float32) * spread * gain
    return jnp.minimum(jnp.maximum(drawn, -reach), reach).astype(held_as)


def setup_inputs(seed: int = 0) -> dict:
    key_list = jax.random.split(jax.random.key(seed), 12)
    fields = noise(key_list[0], (BATCH, SLOTS, TILE, TILE * C), 1.0, 6.0, ((0, 4), (1, 64)))
    ocean_mask = touch_ends((jax.random.randint(key_list[1], (SLOTS, TILE, TILE), 0, 4) < 3).astype(jnp.int32), jax.random.fold_in(key_list[1], 1), 0, 1)
    neighbours = draw_neighbours(jax.random.fold_in(key_list[11], 71), 0)
    dw_kernel = noise(key_list[3], (KS * KS, C), (KS * KS) ** -0.5, 0.875, (), jnp.float32)
    ln_gain = jnp.clip(jnp.exp(jax.random.uniform(key_list[4], (C,), jnp.float32, math.log(0.5), math.log(2.0))), 0.5, 2.0)
    ln_bias = noise(key_list[5], (C,), 0.5, 3.0, (), jnp.float32)
    w_in = noise(key_list[6], (C, HID), C ** -0.5, 0.4375)
    b_in = noise(key_list[7], (HID,), 0.5, 3.0, (), jnp.float32)
    w_out = noise(key_list[8], (HID, C), HID ** -0.5, 0.21875)
    layer_scale = jnp.clip(jnp.exp(jax.random.uniform(key_list[9], (C,), jnp.float32, math.log(0.3), math.log(1.5))), 0.3, 1.5)
    cotangent = noise(key_list[10], (BATCH, SLOTS, TILE, TILE * C), 1.0, 6.0, ((0, 4), (1, 64)))
    return {"fields": fields, "ocean_mask": ocean_mask, "neighbours": neighbours, "dw_kernel": dw_kernel, "ln_gain": ln_gain, "ln_bias": ln_bias, "w_in": w_in, "b_in": b_in, "w_out": w_out, "layer_scale": layer_scale, "cotangent": cotangent}


RIM_FOR_DIRECTION = (0, 0, 0, 2, 3, 1, 1, 1)
INV_SQRT2 = 0.7071067811865476
INV_SQRT_2PI = 0.3989422804014327

def border_rims(tile_set):
    leading = tile_set.shape[:-3]
    tile_len = tile_set.shape[-3]
    width = tile_len * tile_set.shape[-1]
    top_rows = tile_set[..., tile_len - 3:, :, :].reshape(leading + (3, width))
    bottom_rows = tile_set[..., :3, :, :].reshape(leading + (3, width))
    right_cols = jnp.swapaxes(tile_set[..., :, tile_len - 3:, :], -3, -2).reshape(leading + (3, width))
    left_cols = jnp.swapaxes(tile_set[..., :, :3, :], -3, -2).reshape(leading + (3, width))
    return jnp.stack([top_rows, bottom_rows, right_cols, left_cols], axis=-3)

def assemble(tile_set, picked):
    leading = tile_set.shape[:-3]
    tile_len = tile_set.shape[-3]
    channels = tile_set.shape[-1]
    pieces = picked.reshape(leading + (8, 3, tile_len, channels))
    south = jnp.concatenate([pieces[..., 0, :, tile_len - 3:, :], pieces[..., 1, :, :, :], pieces[..., 2, :, :3, :]], axis=-2)
    west_side = jnp.swapaxes(pieces[..., 3, :, :, :], -3, -2)
    east_side = jnp.swapaxes(pieces[..., 4, :, :, :], -3, -2)
    middle = jnp.concatenate([west_side, tile_set, east_side], axis=-2)
    north = jnp.concatenate([pieces[..., 5, :, tile_len - 3:, :], pieces[..., 6, :, :, :], pieces[..., 7, :, :3, :]], axis=-2)
    return jnp.concatenate([south, middle, north], axis=-3)

def extend_tiles(tile_set, neighbours):
    slot_count = tile_set.shape[0]
    borders = border_rims(tile_set)
    width = borders.shape[-1]
    flat_rims = jnp.concatenate([borders.reshape(slot_count * 4, 3, width), jnp.zeros((4, 3, width), tile_set.dtype)], axis=0)
    entries = jnp.where(neighbours < 0, slot_count, neighbours).astype(jnp.int32)
    lookup = entries * 4 + jnp.array(RIM_FOR_DIRECTION, dtype=jnp.int32)
    picked = jnp.take(flat_rims, lookup.reshape(-1), axis=0).reshape(slot_count, 8, 3, width)
    return assemble(tile_set, picked)

def depthwise(padded, kernel, tile_len):
    total = jnp.zeros(padded.shape[:-3] + (tile_len, tile_len, padded.shape[-1]), jnp.float32)
    for row_tap in range(KS):
        for col_tap in range(KS):
            window = padded[..., row_tap:row_tap + tile_len, col_tap:col_tap + tile_len, :]
            total = total + window.astype(jnp.float32) * kernel[KS * row_tap + col_tap]
    return total

def kernel_grad(padded, back_conv, tile_len):
    back_values = back_conv.astype(jnp.float32)
    axes_all = tuple(range(back_values.ndim - 1))
    taps = []
    for row_tap in range(KS):
        for col_tap in range(KS):
            window = padded[..., row_tap:row_tap + tile_len, col_tap:col_tap + tile_len, :]
            taps.append(lax.optimization_barrier(jnp.sum(window.astype(jnp.float32) * back_values, axis=axes_all)))
    return jnp.stack(taps, axis=0)

def contract_rows(left_side, right_side):
    return lax.dot_general(left_side, right_side, (((0,), (0,)), ((), ())), preferred_element_type=jnp.float32)

def contract_cols(left_side, right_side):
    return lax.dot_general(left_side, right_side, (((1,), (1,)), ((), ())), preferred_element_type=jnp.float32)

def mlp_pass(conv_rows, masked_rows, seed_rows, keep_rows, ln_gain, ln_bias, w_in, b_in, w_out, layer_scale):
    mean_val = lax.optimization_barrier(jnp.mean(conv_rows, axis=-1, keepdims=True))
    centred = conv_rows - mean_val
    inv_std = lax.rsqrt(lax.optimization_barrier(jnp.mean(centred * centred, axis=-1, keepdims=True)) + 1e-06)
    normed = centred * inv_std
    shifted = (normed * ln_gain + ln_bias).astype(jnp.bfloat16)
    preact = jnp.dot(shifted, w_in, preferred_element_type=jnp.float32) + b_in
    gelu_cdf = 0.5 * (1.0 + jax.scipy.special.erf(preact * INV_SQRT2))
    hidden = (preact * gelu_cdf).astype(jnp.bfloat16)
    branch = jnp.dot(hidden, w_out, preferred_element_type=jnp.float32)
    result = (keep_rows * (masked_rows.astype(jnp.float32) + layer_scale * branch)).astype(jnp.bfloat16)
    grad_scale_part = lax.optimization_barrier(jnp.sum(seed_rows * branch, axis=0))
    back_branch = (seed_rows * layer_scale).astype(jnp.bfloat16)
    grad_out_part = contract_rows(hidden, back_branch)
    back_hidden = contract_cols(back_branch, w_out)
    density = jnp.exp(-0.5 * preact * preact) * INV_SQRT_2PI
    back_pre = (back_hidden * (gelu_cdf + preact * density)).astype(jnp.bfloat16)
    grad_bias_part = lax.optimization_barrier(jnp.sum(back_pre.astype(jnp.float32), axis=0))
    grad_in_part = contract_rows(shifted, back_pre)
    back_shift = contract_cols(back_pre, w_in)
    grad_gain_part = lax.optimization_barrier(jnp.sum(back_shift * normed, axis=0))
    grad_shift_part = lax.optimization_barrier(jnp.sum(back_shift, axis=0))
    scaled = back_shift * ln_gain
    back_conv = (inv_std * (scaled - lax.optimization_barrier(jnp.mean(scaled, axis=-1, keepdims=True)) - normed * lax.optimization_barrier(jnp.mean(scaled * normed, axis=-1, keepdims=True)))).astype(jnp.bfloat16)
    return (result, back_conv, (grad_gain_part, grad_shift_part, grad_in_part, grad_bias_part, grad_out_part, grad_scale_part))

def reference(fields, ocean_mask, neighbours, dw_kernel, ln_gain, ln_bias, w_in, b_in, w_out, layer_scale, cotangent):
    keep_cells = (ocean_mask > 0)[..., None]
    keep_float = keep_cells.astype(jnp.float32)

    def one_sample(pair):
        field_one, cot_one = pair
        tile_set = field_one.reshape(SLOTS, TILE, TILE, C)
        masked = jnp.where(keep_cells, tile_set, jnp.zeros_like(tile_set))
        padded = extend_tiles(masked, neighbours)
        conv_out = depthwise(padded, dw_kernel, TILE)
        seed_tiles = cot_one.reshape(SLOTS, TILE, TILE, C).astype(jnp.float32) * keep_float

        def one_block(items):
            conv_rows, masked_rows, seed_rows, keep_rows = items
            return mlp_pass(conv_rows, masked_rows, seed_rows, keep_rows, ln_gain, ln_bias, w_in, b_in, w_out, layer_scale)
        result, back_conv, parts = lax.map(one_block, (conv_out.reshape(N_TILES, TPD * TILE * TILE, C), masked.reshape(N_TILES, TPD * TILE * TILE, C), seed_tiles.reshape(N_TILES, TPD * TILE * TILE, C), jnp.broadcast_to(keep_float, (SLOTS, TILE, TILE, 1)).reshape(N_TILES, TPD * TILE * TILE, 1)))
        back_conv = back_conv.reshape(SLOTS, TILE, TILE, C)
        back_padded = extend_tiles(back_conv, neighbours)
        field_grad = (keep_float * (seed_tiles + depthwise(back_padded, dw_kernel[::-1], TILE))).astype(jnp.bfloat16)
        grad_kernel = kernel_grad(padded, back_conv, TILE)
        summed = tuple((lax.optimization_barrier(jnp.sum(part, axis=0)) for part in parts))
        return (result.reshape(SLOTS, TILE, TILE * C), field_grad.reshape(SLOTS, TILE, TILE * C), (grad_kernel,) + summed)
    block_out, field_grad, grads = lax.map(one_sample, (fields, cotangent))
    factor = 1.0 / math.sqrt(CELLS)
    totals = [lax.optimization_barrier(jnp.sum(item, axis=0)) * factor for item in grads]
    return (block_out, field_grad, totals[0], totals[1], totals[2], totals[3], totals[4], totals[5], totals[6])
```

```python
import functools
import math

import jax
import jax.numpy as jnp
from jax import lax
from jax.experimental import pallas as pl
from jax.experimental.pallas import tpu as pltpu
from jax.sharding import PartitionSpec as P

KS = 7
TAPS = KS * KS
TPD = 4
TILE = 16
C = 192
HID = 768
WIDTH = TILE * C
BLOCKS = WIDTH // 128
PAD_BLOCKS = 36
STRIP = 80
CELLS = TILE * TILE
INV_SQRT2 = 0.7071067811865476
INV_SQRT_2PI = 0.3989422804014327
EXTRA = 128
HALF_ROWS = 6 * C + EXTRA // 2
F32 = jnp.float32
BF16 = jnp.bfloat16
VMEM_LIMIT = 20 * 1024 * 1024


def low_lanes(rows):
    return lax.broadcasted_iota(jnp.int32, (rows, 128), 1) < 64


def expand_mask(mask_ref, s):
    cell = lax.broadcasted_iota(jnp.int32, (TILE, WIDTH), 0) * C
    lane = lax.broadcasted_iota(jnp.int32, (TILE, WIDTH), 1)
    spread = jnp.where((lane >= cell) & (lane < cell + C), 1.0, 0.0).astype(BF16)
    keep = (mask_ref[s] > 0).astype(F32).astype(BF16)
    return jnp.dot(keep, spread, preferred_element_type=F32)


def chip_is_even():
    return lax.rem(lax.div(lax.axis_index("tiles"), 2), 2) == 0


def core_is_first():
    return lax.rem(lax.axis_index("tiles"), 2) == 0


def emit_strips(tile_block, strip, early, late, far, right_own, left_own):
    even, first_core = chip_is_even(), core_is_first()
    higher, lower = jnp.where(even, 0, 1), jnp.where(even, 1, 0)

    def put(place, entry, rows, values):
        @pl.when(place == 0)
        def _():
            early[entry, rows, :] = values

        @pl.when(place == 1)
        def _():
            late[entry, rows, :] = values

    everything = slice(0, STRIP)
    strip[72:80, :] = jnp.zeros((8, 128), F32)
    for s in range(TPD):
        for t in range(BLOCKS):
            strip[3 * t : 3 * t + 3, :] = tile_block(s, t, 13, 3)
        top = strip[...].astype(BF16)
        put(higher, s, everything, top)
        for t in range(BLOCKS):
            strip[3 * t : 3 * t + 3, :] = tile_block(s, t, 0, 3)
        bottom = strip[...].astype(BF16)
        put(lower, s, everything, bottom)
        if s == 0:

            @pl.when(first_core)
            def _(bottom=bottom):
                far[0] = bottom

        if s == TPD - 1:

            @pl.when(jnp.logical_not(first_core))
            def _(top=top):
                far[0] = top

        for t in range(5):
            rows = slice(16 * t, 16 * t + 16)
            right = tile_block(s, 19 + t, 0, 16).astype(BF16)
            left = tile_block(s, t, 0, 16).astype(BF16)
            if s == TPD - 1:
                put(higher, TPD, rows, right)
            else:
                right_own[s, rows, :] = right
            if s == 0:
                put(lower, TPD, rows, left)
            else:
                left_own[s - 1, rows, :] = left


def strip_shapes():
    return [jax.ShapeDtypeStruct((n, STRIP, 128), BF16) for n in (TPD + 1, TPD + 1, 1, TPD - 1, TPD - 1)]


def by_chip(early, late, came_early, came_late, work):
    even = chip_is_even()

    @pl.when(even)
    def _():
        work(early, late, came_late, came_early)

    @pl.when(jnp.logical_not(even))
    def _():
        work(late, early, came_early, came_late)


def by_core(first, second):
    is_first = core_is_first()

    @pl.when(is_first)
    def _():
        first()

    @pl.when(jnp.logical_not(is_first))
    def _():
        second()


def relay_kernel(early, late, came_early, came_late, relay):
    def work(own_down, own_up, lower, higher):
        def fill(own, whole, one):
            for n in range(TPD + 1):
                relay[n] = own[n]
                relay[TPD + 1 + n] = whole[n]
            relay[2 * TPD + 2] = one[...]

        by_core(
            lambda: fill(own_down, higher, lower.at[TPD - 1]),
            lambda: fill(own_up, lower, higher.at[0]),
        )

    by_chip(early, late, came_early, came_late, work)


def gather_strips(given, rows_below, rows_above, right_cols, left_cols):
    early, late, right_own, left_own, came_early, came_late, came_far, relay = given
    for s in range(TPD - 1):
        right_cols[1 + s] = right_own[s]
        left_cols[1 + s] = left_own[s]

    def work(own_down, own_up, lower, higher):
        for s in range(TPD):
            rows_below[4 + s] = lower[s]
            rows_below[12 + s] = own_down[s]
            rows_above[s] = own_up[s]
            rows_above[8 + s] = higher[s]
        right_cols[TPD] = own_down[TPD]
        left_cols[0] = own_up[TPD]

    by_chip(early, late, came_early, came_late, work)

    def place(below, above, one_below, one_above):
        rows_below[3] = one_below[...]
        rows_above[12] = one_above[...]
        for s in range(TPD):
            rows_below[8 + s] = relay[below + s]
            rows_above[4 + s] = relay[above + s]
        right_cols[0] = relay[below + TPD]
        left_cols[TPD] = relay[above + TPD]

    last = 2 * TPD + 2
    by_core(
        lambda: place(TPD + 1, 0, came_far.at[0], relay.at[last]),
        lambda: place(0, TPD + 1, relay.at[last], came_far.at[0]),
    )


def fill_halo(padded, shifted, near_ref, strip, edges, tiles):
    rows_below, rows_above, right_cols, left_cols = edges
    first = lax.axis_index("tiles") * TPD

    def one_tile(s, carry):
        tile = tiles[0] + s

        def fetch(direction, source, base, count):
            slot = near_ref[tile, direction]
            place = jnp.clip(slot - first + base, 0, count - 1)
            values = source[place].astype(F32)
            return jnp.where(slot >= 0, values, 0.0)

        def put_rows(values, row, source_block, target_block, count):
            strip[...] = values
            for t in range(count):
                at = 3 * (source_block + t)
                padded[s, target_block + t, row : row + 3, :] = strip[at : at + 3, :]

        put_rows(fetch(1, rows_below, 12, 16), 5, 0, 6, BLOCKS)
        put_rows(fetch(0, rows_below, 12, 16), 5, 19, 1, 5)
        put_rows(fetch(2, rows_below, 12, 16), 5, 0, 30, 5)
        put_rows(fetch(6, rows_above, 0, 16), 24, 0, 6, BLOCKS)
        put_rows(fetch(5, rows_above, 0, 16), 24, 19, 1, 5)
        put_rows(fetch(7, rows_above, 0, 16), 24, 0, 30, 5)
        west = fetch(3, right_cols, 1, TPD + 1)
        east = fetch(4, left_cols, 0, TPD + 1)
        for t in range(5):
            padded[s, 1 + t, 8:24, :] = west[16 * t : 16 * t + 16, :]
            padded[s, 30 + t, 8:24, :] = east[16 * t : 16 * t + 16, :]
        low = low_lanes(32)
        turned = pltpu.roll(padded[s, 1], 64, 1)
        for t in range(1, 34):
            following = pltpu.roll(padded[s, t + 1], 64, 1)
            shifted[s, t] = jnp.where(low, turned, following)
            turned = following
        return carry

    lax.fori_loop(0, len(tiles), one_tile, 0)


def spread_taps(dw_ref, wide, taps):
    low = low_lanes(TAPS)
    first = dw_ref[:, 0:128]
    last = dw_ref[:, 64:192]
    wide[0, 0:TAPS, :] = first
    turned_first = pltpu.roll(first, 64, 1)
    turned_last = pltpu.roll(last, 64, 1)
    wide[1, 0:TAPS, :] = jnp.where(low, turned_last, turned_first)
    wide[2, 0:TAPS, :] = last
    for k in range(TAPS):
        for m in range(3):
            taps[3 * k + m] = jnp.broadcast_to(wide[m, k : k + 1, :], (8, 128))


def windows(padded, shifted, s, m, row):
    half = BLOCKS // 3
    even = [shifted[s, 1 + m + 3 * n, pl.ds(row, 8), :] for n in range(half + 3)]
    odd = [padded[s, 3 + m + 3 * n, pl.ds(row, 8), :] for n in range(half + 2)]
    return lambda q, j: (odd if j % 2 else even)[q + j // 2]


def depthwise(padded, shifted, taps, out, flip, count=TPD):
    half = BLOCKS // 3
    for m in range(3):

        def body(s, carry, m=m):
            for h in range(2):
                total = [None] * half
                for i in range(KS):
                    window = windows(padded, shifted, s, m, 5 + i + 8 * h)
                    for j in range(KS):
                        k = KS * i + j
                        weight = taps[3 * (TAPS - 1 - k if flip else k) + m]
                        for q in range(half):
                            term = window(q, j) * weight
                            total[q] = term if total[q] is None else total[q] + term
                for q in range(half):
                    out[s, 3 * q + m, 8 * h : 8 * h + 8, :] = total[q]
            return carry

        lax.fori_loop(0, count, body, 0)


def kernel_grad(padded, shifted, back, wide):
    half = BLOCKS // 3
    for m in range(3):
        for i in range(KS):

            def body(s, totals, m=m, i=i):
                totals = list(totals)
                for h in range(2):
                    window = windows(padded, shifted, s, m, 5 + i + 8 * h)
                    here = [back[s, 3 * q + m, 8 * h : 8 * h + 8, :] for q in range(half)]
                    for j in range(KS):
                        for q in range(half):
                            totals[j] = totals[j] + window(q, j) * here[q]
                return tuple(totals)

            start = tuple(jnp.zeros((8, 128), F32) for _ in range(KS))
            totals = lax.fori_loop(0, TPD, body, start)
            for j in range(KS):
                k = KS * i + j
                wide[m, k : k + 1, :] = jnp.sum(totals[j], axis=0, keepdims=True)


def to_rows(block, rows_ref):
    low = low_lanes(TILE)
    for q in range(TILE // 2):
        first, middle, last = block(3 * q), block(3 * q + 1), block(3 * q + 2)
        even = slice(32 * q, 32 * q + 16)
        odd = slice(32 * q + 16, 32 * q + 32)
        rows_ref[even, 0:128] = first
        rows_ref[even, 128:256] = middle
        turned = pltpu.roll(last, 64, 1)
        rows_ref[odd, 0:128] = jnp.where(low, pltpu.roll(middle, 64, 1), turned)
        rows_ref[odd, 128:256] = turned


def from_rows(rows_ref, put):
    low = low_lanes(TILE)
    for q in range(TILE // 2):
        even = slice(32 * q, 32 * q + 16)
        odd = slice(32 * q + 16, 32 * q + 32)
        turned = pltpu.roll(rows_ref[odd, 0:128], 64, 1)
        put(3 * q, rows_ref[even, 0:128])
        put(3 * q + 1, jnp.where(low, rows_ref[even, 128:256], turned))
        put(3 * q + 2, jnp.where(low, turned, pltpu.roll(rows_ref[odd, 128:256], 64, 1)))


def dot_last(left, right):
    return lax.dot_general(left, right, (((1,), (1,)), ((), ())), preferred_element_type=F32)


def dot_first(left, right):
    return lax.dot_general(left, right, (((0,), (0,)), ((), ())), preferred_element_type=F32)


def prepare_kernel(fields_far, mask_far, *refs):
    strips, (blocks, strip, fields, mask, sems) = refs[0:5], refs[5:]
    copies = [
        pltpu.make_async_copy(fields_far, fields, sems.at[0]),
        pltpu.make_async_copy(mask_far, mask, sems.at[1]),
    ]
    for copy in copies:
        copy.start()
    for copy in copies:
        copy.wait()
    for s in range(TPD):
        keep = expand_mask(mask, s) > 0.5
        values = jnp.where(keep, fields[s].astype(F32), 0.0)
        for t in range(BLOCKS):
            blocks[s, t] = values[:, 128 * t : 128 * t + 128]
    emit_strips(lambda s, t, row, rows: blocks[s, t, row : row + rows, :], strip, *strips)


def block_kernel(*refs):
    fields, cotangent, mask, near, dw, gain_ref, bias_ref, w_in_far, b_in, w_out_far, scale_ref = refs[0:11]
    given = refs[11:19]
    block_out, back_out, keep_rows, send_rows = refs[19:23]
    strips = refs[23:28]
    (
        padded, shifted_pad, keep_blocks, blocks, strip, rows_below, rows_above, right_cols, left_cols,
        wide, taps, rows_a, rows_b, norm_rows, hid_rows, bb_rows, pre_rows, sums, bias_sums, extra,
        w_in, w_out, weight_sems,
    ) = refs[28:]

    arrive_in = pltpu.make_async_copy(w_in_far, w_in, weight_sems.at[0])
    arrive_out = pltpu.make_async_copy(w_out_far, w_out, weight_sems.at[1])
    arrive_in.start()
    arrive_out.start()
    for s in range(TPD):
        keep = expand_mask(mask, s)
        values = jnp.where(keep > 0.5, fields[s].astype(F32), 0.0)
        for t in range(BLOCKS):
            padded[s, 6 + t, 8:24, :] = values[:, 128 * t : 128 * t + 128]
            keep_blocks[s, t] = keep[:, 128 * t : 128 * t + 128]
    spread_taps(dw, wide, taps)
    gather_strips(given, rows_below, rows_above, right_cols, left_cols)
    edges = (rows_below, rows_above, right_cols, left_cols)
    fill_halo(padded, shifted_pad, near, strip, edges, range(TPD))
    depthwise(padded, shifted_pad, taps, blocks, False)
    arrive_in.wait()
    arrive_out.wait()

    sums[...] = jnp.zeros_like(sums)
    bias_sums[...] = jnp.zeros_like(bias_sums)

    def one_tile(s, carry):
        gain, scale = gain_ref[...], scale_ref[...]
        to_rows(lambda t: blocks[s, t], rows_a)
        to_rows(
            lambda t: cotangent[s, :, 128 * t : 128 * t + 128].astype(F32) * keep_blocks[s, t], rows_b
        )
        conv = rows_a[:, 0:C]
        seed = rows_b[:, 0:C]
        centred = conv - jnp.mean(conv, axis=-1, keepdims=True)
        inv_std = lax.rsqrt(jnp.mean(centred * centred, axis=-1, keepdims=True) + 1e-06)
        normed = centred * inv_std
        shifted = (normed * gain + bias_ref[...]).astype(BF16)
        norm_rows[s] = shifted
        preact = jnp.dot(shifted, w_in[...], preferred_element_type=F32) + b_in[...]
        bell = jnp.exp(-0.5 * preact * preact)
        u = 1.0 / (1.0 + (0.3275911 * INV_SQRT2) * jnp.abs(preact))
        series = u * (
            0.5 * 0.254829592
            + u * (0.5 * -0.284496736 + u * (0.5 * 1.421413741 + u * (0.5 * -1.453152027 + u * (0.5 * 1.061405429))))
        )
        tail = series * bell
        cdf = jnp.where(preact >= 0.0, 1.0 - tail, tail)
        hidden = (preact * cdf).astype(BF16)
        hid_rows[s] = hidden
        slope = cdf + preact * bell * INV_SQRT_2PI
        branch = dot_last(hidden, w_out[...])
        rows_a[:, 0:C] = branch * scale

        def put_out(t, values):
            total = padded[s, 6 + t, 8:24, :] + values
            block_out[s, :, 128 * t : 128 * t + 128] = (keep_blocks[s, t] * total).astype(BF16)

        from_rows(rows_a, put_out)
        sums[0:1, 0:C] += jnp.sum(seed * branch, axis=0, keepdims=True)
        back_branch = (seed * scale).astype(BF16)
        bb_rows[s] = back_branch
        back_pre = (jnp.dot(back_branch, w_out[...], preferred_element_type=F32) * slope).astype(BF16)
        pre_rows[s] = back_pre
        bias_sums[...] += jnp.sum(back_pre.astype(F32), axis=0, keepdims=True)
        back_shift = dot_last(back_pre, w_in[...])
        sums[1:2, 0:C] += jnp.sum(back_shift * normed, axis=0, keepdims=True)
        sums[2:3, 0:C] += jnp.sum(back_shift, axis=0, keepdims=True)
        scaled = back_shift * gain
        back = inv_std * (
            scaled
            - jnp.mean(scaled, axis=-1, keepdims=True)
            - normed * jnp.mean(scaled * normed, axis=-1, keepdims=True)
        )
        rows_b[:, 0:C] = back.astype(BF16).astype(F32)

        def put_back(t, values):
            blocks[s, t] = values
            back_out[s, :, 128 * t : 128 * t + 128] = values.astype(BF16)

        from_rows(rows_b, put_back)
        return carry

    lax.fori_loop(0, TPD, one_tile, 0)

    emit_strips(lambda s, t, row, rows: blocks[s, t, row : row + rows, :], strip, *strips)
    kernel_grad(padded, shifted_pad, blocks, wide)
    low = low_lanes(TAPS)
    first, middle, last = wide[0, 0:TAPS, :], wide[1, 0:TAPS, :], wide[2, 0:TAPS, :]
    turned_middle, turned_last = pltpu.roll(middle, 64, 1), pltpu.roll(last, 64, 1)
    extra[...] = jnp.zeros_like(extra)
    extra[0:TAPS, :] = first + jnp.where(low, turned_middle, turned_last)
    extra[56 : 56 + TAPS, :] = jnp.where(low, middle + turned_last, 0.0)
    for n in range(3):
        extra[112 + 2 * n : 113 + 2 * n, :] = sums[n : n + 1, 0:128]
        extra[113 + 2 * n : 114 + 2 * n, :] = sums[n : n + 1, 128:256]
    for n in range(6):
        extra[118 + n : 119 + n, :] = bias_sums[0:1, 128 * n : 128 * n + 128]
    grad_in = dot_first(norm_rows[...].reshape(TPD * CELLS, C), pre_rows[...].reshape(TPD * CELLS, HID))
    grad_out = dot_first(bb_rows[...].reshape(TPD * CELLS, C), hid_rows[...].reshape(TPD * CELLS, HID))
    core = lax.rem(lax.axis_index("tiles"), 2)

    def write(target, grad, part, kind):
        for n in range(6):
            target[C * n : C * n + C, :] = grad[:, 128 * n : 128 * n + 128].astype(kind)
        target[6 * C : HALF_ROWS, :] = extra[part * (EXTRA // 2) : (part + 1) * (EXTRA // 2), :].astype(kind)

    @pl.when(core == 0)
    def _():
        write(keep_rows, grad_in, 0, F32)
        write(send_rows, grad_out, 1, BF16)

    @pl.when(core == 1)
    def _():
        write(keep_rows, grad_out, 1, F32)
        write(send_rows, grad_in, 0, BF16)


def field_grad_kernel(tile, *refs):
    back, cotangent, mask, near, dw = refs[0:5]
    given, out = refs[5:13], refs[13]
    padded, shifted_pad, blocks, strip, rows_below, rows_above, right_cols, left_cols, wide, taps = refs[14:]
    for t in range(BLOCKS):
        padded[0, 6 + t, 8:24, :] = back[tile, :, 128 * t : 128 * t + 128].astype(F32)
    spread_taps(dw, wide, taps)
    gather_strips(given, rows_below, rows_above, right_cols, left_cols)
    edges = (rows_below, rows_above, right_cols, left_cols)
    fill_halo(padded, shifted_pad, near, strip, edges, range(tile, tile + 1))
    depthwise(padded, shifted_pad, taps, blocks, True, 1)
    keep = expand_mask(mask, tile)
    for t in range(BLOCKS):
        lanes = slice(128 * t, 128 * t + 128)
        total = cotangent[tile, :, lanes].astype(F32) + blocks[0, t]
        out[0, :, lanes] = (keep[:, lanes] * total).astype(BF16)


def unpack_kernel(rows, grad_kernel, gain, shift, grad_in, bias, grad_out, scale):
    factor = 1.0 / math.sqrt(4 * 64 * TPD * CELLS)

    for n in range(6):
        grad_in[:, 128 * n : 128 * n + 128] = rows[C * n : C * n + C, :].astype(F32) * factor
        at = HALF_ROWS + C * n
        grad_out[:, 128 * n : 128 * n + 128] = rows[at : at + C, :].astype(F32) * factor
    first_part = rows[6 * C : HALF_ROWS, :].astype(F32) * factor
    last_part = rows[HALF_ROWS + 6 * C :, :].astype(F32) * factor
    grad_kernel[:, 0:128] = first_part[0:TAPS, :]
    both = jnp.concatenate([first_part[56:64, :], last_part[0:48, :]], axis=0)
    grad_kernel[:, 128:192] = both[0:TAPS, 0:64]
    tail = last_part[48:64, :]
    for n, target in ((0, scale), (1, gain), (2, shift)):
        target[:, 0:128] = tail[2 * n : 2 * n + 1, :]
        target[:, 128:192] = tail[2 * n + 1 : 2 * n + 2, 0:64]
    for n in range(6):
        bias[128 * n : 128 * n + 128] = tail[6 + n, :]


def whole(memory=pltpu.VMEM):
    return pl.BlockSpec(memory_space=memory)


def call(kernel, inputs, out_shape, scratch, cost, smem=(), far=()):
    place = lambda n: pltpu.SMEM if n in smem else pl.ANY if n in far else pltpu.VMEM
    return pl.pallas_call(
        kernel,
        out_shape=out_shape,
        in_specs=[whole(place(n)) for n in range(len(inputs))],
        out_specs=jax.tree.map(lambda _: whole(), out_shape),
        scratch_shapes=scratch,
        compiler_params=pltpu.CompilerParams(vmem_limit_bytes=VMEM_LIMIT),
        cost_estimate=pl.CostEstimate(flops=cost, bytes_accessed=4000000, transcendentals=0),
    )(*inputs)


def halo_scratch():
    return [
        pltpu.VMEM((STRIP, 128), F32),
        pltpu.VMEM((16, STRIP, 128), BF16),
        pltpu.VMEM((16, STRIP, 128), BF16),
        pltpu.VMEM((TPD + 1, STRIP, 128), BF16),
        pltpu.VMEM((TPD + 1, STRIP, 128), BF16),
    ]


def swap(block, axis, partner):
    count = lax.axis_size(axis)
    return lax.ppermute(block, axis, [(i, partner(i)) for i in range(count) if 0 <= partner(i) < count])


def chip_up(i):
    return i ^ 2


def chip_down(i):
    return ((i // 2 + 1) ^ 1) * 2 - 2 + i % 2


def three_away(i):
    return i + 3 if i % 2 else i - 3


def other_core(i):
    return i ^ 1


def relay(early, late, came_early, came_late):
    shape = jax.ShapeDtypeStruct((2 * TPD + 3, STRIP, 128), BF16)
    return call(relay_kernel, (early, late, came_early, came_late), shape, [], 10**5)


def exchange_strips(strips):
    early, late, far, right_own, left_own = strips
    came_early = swap(early, "tiles", chip_up)
    came_late = swap(late, "tiles", chip_down)
    came_far = swap(far, "tiles", three_away)
    passed = swap(relay(early, late, came_early, came_late), "tiles", other_core)
    return (early, late, right_own, left_own, came_early, came_late, came_far, passed)


def reduce_and_exchange(keep, send, strips, finish):
    early, late, far, right_own, left_own = strips
    place = lax.axis_index("tiles")
    core, y = place % 2, (place // 2) % 4
    x = lax.axis_index("dp")

    def halves(block, bit):
        n = block.shape[0] // 2
        own = lax.dynamic_slice_in_dim(block, bit * n, n, 0)
        return own, lax.dynamic_slice_in_dim(block, (1 - bit) * n, n, 0).astype(BF16)

    def join(block, axis, partner, bit):
        other = swap(block, axis, partner)
        return jnp.where(bit == 0, jnp.concatenate([block, other], 0), jnp.concatenate([other, block], 0))

    first_x, second_x, first_y = (x + x // 2) % 2, x // 2, (y + y // 2) % 2
    came, came_early = lax.optimization_barrier((swap(send, "tiles", other_core), swap(early, "tiles", chip_up)))
    own, other = halves(keep + came.astype(F32), first_x)
    came, came_late = lax.optimization_barrier((swap(other, "dp", lambda i: i ^ 1), swap(late, "tiles", chip_down)))
    own, other = halves(own + came.astype(F32), second_x)
    between = relay(early, late, came_early, came_late)
    came, passed = lax.optimization_barrier((swap(other, "dp", lambda i: i ^ 3), swap(between, "tiles", other_core)))
    own, other = halves(own + came.astype(F32), first_y)
    came, came_far = lax.optimization_barrier((swap(other, "tiles", lambda i: i ^ 2), swap(far, "tiles", three_away)))
    mine = own + came.astype(F32)
    given = (early, late, right_own, left_own, came_early, came_late, came_far, passed)
    parts = []
    for tile, mask in enumerate((6, 8, 24, 56)):
        sent, given = lax.optimization_barrier((mine.astype(BF16), given))
        came, part = lax.optimization_barrier((swap(sent, "tiles", lambda i: i ^ mask), finish(tile, given)))
        parts.append(part)
        mine = sent.astype(F32) + came.astype(F32)
    mine = mine.astype(BF16)
    mine = join(mine, "tiles", lambda i: i ^ 2, first_y)
    mine = join(mine, "dp", lambda i: i ^ 3, second_x)
    mine = join(mine, "dp", lambda i: i ^ 1, first_x)
    return join(mine, "tiles", other_core, core), jnp.concatenate(parts, 0)


def shards(
    fields, ocean_mask, neighbours, dw_kernel, ln_gain, ln_bias, w_in, b_in, w_out, layer_scale, cotangent
):
    tiles = fields.reshape(TPD, TILE, WIDTH)
    cot = cotangent.reshape(TPD, TILE, WIDTH)
    tile_shape = jax.ShapeDtypeStruct((TPD, TILE, WIDTH), BF16)
    block_scratch = pltpu.VMEM((TPD, BLOCKS, TILE, 128), F32)
    pad_scratch = pltpu.VMEM((TPD, PAD_BLOCKS, 32, 128), F32)
    tap_scratch = [pltpu.VMEM((3, 56, 128), F32), pltpu.VMEM((3 * TAPS, 8, 128), F32)]

    strips = call(
        prepare_kernel,
        (tiles, ocean_mask),
        strip_shapes(),
        [
            block_scratch,
            pltpu.VMEM((STRIP, 128), F32),
            pltpu.VMEM((TPD, TILE, WIDTH), BF16),
            pltpu.VMEM((TPD, TILE, TILE), jnp.int32),
            pltpu.SemaphoreType.DMA((2,)),
        ],
        10**6,
        far=(0, 1),
    )
    given = exchange_strips(strips)
    row = lambda v: v.reshape(1, -1)
    outs = call(
        block_kernel,
        (
            tiles, cot, ocean_mask, neighbours, dw_kernel, row(ln_gain), row(ln_bias), w_in, row(b_in), w_out.T,
            row(layer_scale), *given,
        ),
        [
            tile_shape,
            tile_shape,
            jax.ShapeDtypeStruct((HALF_ROWS, 128), F32),
            jax.ShapeDtypeStruct((HALF_ROWS, 128), BF16),
            *strip_shapes(),
        ],
        [
            pad_scratch, pad_scratch, block_scratch, block_scratch, *halo_scratch(), *tap_scratch,
            pltpu.VMEM((CELLS, 256), F32),
            pltpu.VMEM((CELLS, 256), F32),
            pltpu.VMEM((TPD, CELLS, C), BF16),
            pltpu.VMEM((TPD, CELLS, HID), BF16),
            pltpu.VMEM((TPD, CELLS, C), BF16),
            pltpu.VMEM((TPD, CELLS, HID), BF16),
            pltpu.VMEM((8, 256), F32),
            pltpu.VMEM((1, HID), F32),
            pltpu.VMEM((EXTRA, 128), F32),
            pltpu.VMEM((C, HID), BF16),
            pltpu.VMEM((C, HID), BF16),
            pltpu.SemaphoreType.DMA((2,)),
        ],
        2 * 10**9,
        smem=(3,),
        far=(7, 9),
    )
    block_out, back, keep_rows, send_rows = outs[0:4]

    def finish(tile, given):
        return call(
            functools.partial(field_grad_kernel, tile),
            (back, cot, ocean_mask, neighbours, dw_kernel, *given),
            jax.ShapeDtypeStruct((1, TILE, WIDTH), BF16),
            [
                pltpu.VMEM((1, PAD_BLOCKS, 32, 128), F32),
                pltpu.VMEM((1, PAD_BLOCKS, 32, 128), F32),
                pltpu.VMEM((1, BLOCKS, TILE, 128), F32),
                *halo_scratch(),
                *tap_scratch,
            ],
            10**9,
            smem=(3,),
        )

    rows, field_grad = reduce_and_exchange(keep_rows, send_rows, outs[4:], finish)
    grads = call(
        unpack_kernel,
        (rows,),
        [
            jax.ShapeDtypeStruct(shape, F32)
            for shape in ((TAPS, C), (1, C), (1, C), (C, HID), (HID,), (C, HID), (1, C))
        ],
        [],
        10**6,
    )
    grad_kernel, gain, shift, grad_in, bias, grad_out, scale = grads
    return (
        block_out.reshape(fields.shape),
        field_grad.reshape(fields.shape),
        grad_kernel,
        gain.reshape(-1),
        shift.reshape(-1),
        grad_in,
        bias,
        grad_out.T,
        scale.reshape(-1),
    )


def solution(mesh):
    cells = P("dp", "tiles", None, None)
    in_specs = (cells, P("tiles", None, None), P("tiles", None)) + (P(),) * 7 + (cells,)
    out_specs = (cells, cells) + (P(),) * 7
    return jax.shard_map(shards, mesh=mesh, in_specs=in_specs, out_specs=out_specs, check_vma=False)
```

```python
import functools
import math

import jax
import jax.numpy as jnp
from jax import lax
from jax.experimental import pallas as pl
from jax.experimental.pallas import tpu as pltpu
from jax.sharding import PartitionSpec as P

KS = 7
TAPS = KS * KS
TPD = 4
TILE = 16
C = 192
HID = 768
WIDTH = TILE * C
BLOCKS = WIDTH // 128
PAD_BLOCKS = 36
STRIP = 80
CELLS = TILE * TILE
INV_SQRT2 = 0.7071067811865476
INV_SQRT_2PI = 0.3989422804014327
EXTRA = 128
HALF_ROWS = 6 * C + EXTRA // 2
F32 = jnp.float32
BF16 = jnp.bfloat16
VMEM_LIMIT = 20 * 1024 * 1024


def low_lanes(rows):
    return lax.broadcasted_iota(jnp.int32, (rows, 128), 1) < 64


def expand_mask(mask_ref, s):
    cell = lax.broadcasted_iota(jnp.int32, (TILE, WIDTH), 0) * C
    lane = lax.broadcasted_iota(jnp.int32, (TILE, WIDTH), 1)
    spread = jnp.where((lane >= cell) & (lane < cell + C), 1.0, 0.0).astype(BF16)
    keep = (mask_ref[s] > 0).astype(F32).astype(BF16)
    return jnp.dot(keep, spread, preferred_element_type=F32)


def up_comes_first():
    return lax.rem(lax.div(lax.axis_index("tiles"), 2), 2) == 0


def core_is_first():
    return lax.rem(lax.axis_index("tiles"), 2) == 0


def emit_strips(tile_block, strip, early, late, far, right_own, left_own):
    even, first_core = up_comes_first(), core_is_first()
    higher, lower = jnp.where(even, 0, 1), jnp.where(even, 1, 0)

    def put(place, entry, rows, values):
        @pl.when(place == 0)
        def _():
            early[entry, rows, :] = values

        @pl.when(place == 1)
        def _():
            late[entry, rows, :] = values

    everything = slice(0, STRIP)
    strip[72:80, :] = jnp.zeros((8, 128), F32)
    for s in range(TPD):
        for t in range(BLOCKS):
            strip[3 * t : 3 * t + 3, :] = tile_block(s, t, 13, 3)
        top = strip[...].astype(BF16)
        put(higher, s, everything, top)
        for t in range(BLOCKS):
            strip[3 * t : 3 * t + 3, :] = tile_block(s, t, 0, 3)
        bottom = strip[...].astype(BF16)
        put(lower, s, everything, bottom)
        if s == 0:

            @pl.when(first_core)
            def _(bottom=bottom):
                far[0] = bottom

        if s == TPD - 1:

            @pl.when(jnp.logical_not(first_core))
            def _(top=top):
                far[0] = top

        for t in range(5):
            rows = slice(16 * t, 16 * t + 16)
            right = tile_block(s, 19 + t, 0, 16).astype(BF16)
            left = tile_block(s, t, 0, 16).astype(BF16)
            if s == TPD - 1:
                put(higher, TPD, rows, right)
            else:
                right_own[s, rows, :] = right
            if s == 0:
                put(lower, TPD, rows, left)
            else:
                left_own[s - 1, rows, :] = left


def strip_shapes():
    return [jax.ShapeDtypeStruct((n, STRIP, 128), BF16) for n in (TPD + 1, TPD + 1, 1, TPD - 1, TPD - 1)]


def by_chip(early, late, came_early, came_late, work):
    even = up_comes_first()

    @pl.when(even)
    def _():
        work(early, late, came_late, came_early)

    @pl.when(jnp.logical_not(even))
    def _():
        work(late, early, came_early, came_late)


def by_core(first, second):
    is_first = core_is_first()

    @pl.when(is_first)
    def _():
        first()

    @pl.when(jnp.logical_not(is_first))
    def _():
        second()


def relay_kernel(early, late, came_early, came_late, relay):
    def work(own_down, own_up, lower, higher):
        def fill(own, whole, one):
            for n in range(TPD + 1):
                relay[n] = own[n]
                relay[TPD + 1 + n] = whole[n]
            relay[2 * TPD + 2] = one[...]

        by_core(
            lambda: fill(own_down, higher, lower.at[TPD - 1]),
            lambda: fill(own_up, lower, higher.at[0]),
        )

    by_chip(early, late, came_early, came_late, work)


def gather_strips(given, rows_below, rows_above, right_cols, left_cols):
    early, late, right_own, left_own, came_early, came_late, came_far, relay = given
    for s in range(TPD - 1):
        right_cols[1 + s] = right_own[s]
        left_cols[1 + s] = left_own[s]

    def work(own_down, own_up, lower, higher):
        for s in range(TPD):
            rows_below[4 + s] = lower[s]
            rows_below[12 + s] = own_down[s]
            rows_above[s] = own_up[s]
            rows_above[8 + s] = higher[s]
        right_cols[TPD] = own_down[TPD]
        left_cols[0] = own_up[TPD]

    by_chip(early, late, came_early, came_late, work)

    def place(below, above, one_below, one_above):
        rows_below[3] = one_below[...]
        rows_above[12] = one_above[...]
        for s in range(TPD):
            rows_below[8 + s] = relay[below + s]
            rows_above[4 + s] = relay[above + s]
        right_cols[0] = relay[below + TPD]
        left_cols[TPD] = relay[above + TPD]

    last = 2 * TPD + 2
    by_core(
        lambda: place(TPD + 1, 0, came_far.at[0], relay.at[last]),
        lambda: place(0, TPD + 1, relay.at[last], came_far.at[0]),
    )


def fill_halo(padded, shifted, near_ref, strip, edges, tiles):
    rows_below, rows_above, right_cols, left_cols = edges
    first = lax.axis_index("tiles") * TPD

    def one_tile(s, carry):
        tile = tiles[0] + s

        def fetch(direction, source, base, count):
            slot = near_ref[tile, direction]
            place = jnp.clip(slot - first + base, 0, count - 1)
            values = source[place].astype(F32)
            return jnp.where(slot >= 0, values, 0.0)

        def put_rows(values, row, source_block, target_block, count):
            strip[...] = values
            for t in range(count):
                at = 3 * (source_block + t)
                padded[s, target_block + t, row : row + 3, :] = strip[at : at + 3, :]

        put_rows(fetch(1, rows_below, 12, 16), 5, 0, 6, BLOCKS)
        put_rows(fetch(0, rows_below, 12, 16), 5, 19, 1, 5)
        put_rows(fetch(2, rows_below, 12, 16), 5, 0, 30, 5)
        put_rows(fetch(6, rows_above, 0, 16), 24, 0, 6, BLOCKS)
        put_rows(fetch(5, rows_above, 0, 16), 24, 19, 1, 5)
        put_rows(fetch(7, rows_above, 0, 16), 24, 0, 30, 5)
        west = fetch(3, right_cols, 1, TPD + 1)
        east = fetch(4, left_cols, 0, TPD + 1)
        for t in range(5):
            padded[s, 1 + t, 8:24, :] = west[16 * t : 16 * t + 16, :]
            padded[s, 30 + t, 8:24, :] = east[16 * t : 16 * t + 16, :]
        low = low_lanes(32)
        turned = pltpu.roll(padded[s, 1], 64, 1)
        for t in range(1, 34):
            following = pltpu.roll(padded[s, t + 1], 64, 1)
            shifted[s, t] = jnp.where(low, turned, following)
            turned = following
        return carry

    lax.fori_loop(0, len(tiles), one_tile, 0)


def spread_taps(dw_ref, wide, taps):
    low = low_lanes(TAPS)
    first = dw_ref[:, 0:128]
    last = dw_ref[:, 64:192]
    wide[0, 0:TAPS, :] = first
    turned_first = pltpu.roll(first, 64, 1)
    turned_last = pltpu.roll(last, 64, 1)
    wide[1, 0:TAPS, :] = jnp.where(low, turned_last, turned_first)
    wide[2, 0:TAPS, :] = last
    for k in range(TAPS):
        for m in range(3):
            taps[3 * k + m] = jnp.broadcast_to(wide[m, k : k + 1, :], (8, 128))


def windows(padded, shifted, s, m, row):
    half = BLOCKS // 3
    even = [shifted[s, 1 + m + 3 * n, pl.ds(row, 8), :] for n in range(half + 3)]
    odd = [padded[s, 3 + m + 3 * n, pl.ds(row, 8), :] for n in range(half + 2)]
    return lambda q, j: (odd if j % 2 else even)[q + j // 2]


def depthwise(padded, shifted, taps, out, flip, count=TPD):
    half = BLOCKS // 3
    for m in range(3):

        def body(s, carry, m=m):
            for h in range(2):
                total = [None] * half
                for i in range(KS):
                    window = windows(padded, shifted, s, m, 5 + i + 8 * h)
                    for j in range(KS):
                        k = KS * i + j
                        weight = taps[3 * (TAPS - 1 - k if flip else k) + m]
                        for q in range(half):
                            term = window(q, j) * weight
                            total[q] = term if total[q] is None else total[q] + term
                for q in range(half):
                    out[s, 3 * q + m, 8 * h : 8 * h + 8, :] = total[q]
            return carry

        lax.fori_loop(0, count, body, 0)


def kernel_grad(padded, shifted, back, wide):
    half = BLOCKS // 3
    for m in range(3):
        for i in range(KS):

            def body(s, totals, m=m, i=i):
                totals = list(totals)
                for h in range(2):
                    window = windows(padded, shifted, s, m, 5 + i + 8 * h)
                    here = [back[s, 3 * q + m, 8 * h : 8 * h + 8, :] for q in range(half)]
                    for j in range(KS):
                        for q in range(half):
                            totals[j] = totals[j] + window(q, j) * here[q]
                return tuple(totals)

            start = tuple(jnp.zeros((8, 128), F32) for _ in range(KS))
            totals = lax.fori_loop(0, TPD, body, start)
            for j in range(KS):
                k = KS * i + j
                wide[m, k : k + 1, :] = jnp.sum(totals[j], axis=0, keepdims=True)


def to_rows(block, rows_ref):
    low = low_lanes(TILE)
    for q in range(TILE // 2):
        first, middle, last = block(3 * q), block(3 * q + 1), block(3 * q + 2)
        even = slice(32 * q, 32 * q + 16)
        odd = slice(32 * q + 16, 32 * q + 32)
        rows_ref[even, 0:128] = first
        rows_ref[even, 128:256] = middle
        turned = pltpu.roll(last, 64, 1)
        rows_ref[odd, 0:128] = jnp.where(low, pltpu.roll(middle, 64, 1), turned)
        rows_ref[odd, 128:256] = turned


def from_rows(rows_ref, put):
    low = low_lanes(TILE)
    for q in range(TILE // 2):
        even = slice(32 * q, 32 * q + 16)
        odd = slice(32 * q + 16, 32 * q + 32)
        turned = pltpu.roll(rows_ref[odd, 0:128], 64, 1)
        put(3 * q, rows_ref[even, 0:128])
        put(3 * q + 1, jnp.where(low, rows_ref[even, 128:256], turned))
        put(3 * q + 2, jnp.where(low, turned, pltpu.roll(rows_ref[odd, 128:256], 64, 1)))


def dot_last(left, right):
    return lax.dot_general(left, right, (((1,), (1,)), ((), ())), preferred_element_type=F32)


def dot_first(left, right):
    return lax.dot_general(left, right, (((0,), (0,)), ((), ())), preferred_element_type=F32)


def prepare_kernel(fields, mask, *refs):
    strips, (blocks, strip) = refs[0:5], refs[5:]
    for s in range(TPD):
        keep = expand_mask(mask, s) > 0.5
        values = jnp.where(keep, fields[s].astype(F32), 0.0)
        for t in range(BLOCKS):
            blocks[s, t] = values[:, 128 * t : 128 * t + 128]
    emit_strips(lambda s, t, row, rows: blocks[s, t, row : row + rows, :], strip, *strips)


def block_kernel(*refs):
    fields, cotangent, mask, near, dw, gain_ref, bias_ref, weights, b_in, scale_ref = refs[0:10]
    given = refs[10:18]
    block_out, back_out, keep_rows, send_rows = refs[18:22]
    strips = refs[22:27]
    w_in, w_out = weights.at[0:C], weights.at[C : 2 * C]
    (
        padded, shifted_pad, keep_blocks, blocks, strip, rows_below, rows_above, right_cols, left_cols,
        wide, taps, rows_a_all, rows_b_all, norm_rows, hid_rows, bb_rows, pre_rows, sums, bias_sums, extra,
    ) = refs[27:]

    for s in range(TPD):
        keep = expand_mask(mask, s)
        values = jnp.where(keep > 0.5, fields[s].astype(F32), 0.0)
        for t in range(BLOCKS):
            padded[s, 6 + t, 8:24, :] = values[:, 128 * t : 128 * t + 128]
            keep_blocks[s, t] = keep[:, 128 * t : 128 * t + 128]
    spread_taps(dw, wide, taps)
    gather_strips(given, rows_below, rows_above, right_cols, left_cols)
    edges = (rows_below, rows_above, right_cols, left_cols)
    fill_halo(padded, shifted_pad, near, strip, edges, range(TPD))
    depthwise(padded, shifted_pad, taps, blocks, False)

    sums[...] = jnp.zeros_like(sums)
    bias_sums[...] = jnp.zeros_like(bias_sums)

    def one_tile(s, carry):
        rows_a, rows_b = rows_a_all.at[s], rows_b_all.at[s]
        gain, scale = gain_ref[...], scale_ref[...]
        to_rows(lambda t: blocks[s, t], rows_a)
        to_rows(
            lambda t: cotangent[s, :, 128 * t : 128 * t + 128].astype(F32) * keep_blocks[s, t], rows_b
        )
        conv = rows_a[:, 0:C]
        seed = rows_b[:, 0:C]
        centred = conv - jnp.mean(conv, axis=-1, keepdims=True)
        inv_std = lax.rsqrt(jnp.mean(centred * centred, axis=-1, keepdims=True) + 1e-06)
        normed = centred * inv_std
        shifted = (normed * gain + bias_ref[...]).astype(BF16)
        norm_rows[s] = shifted
        preact = jnp.dot(shifted, w_in[...], preferred_element_type=F32) + b_in[...]
        bell = jnp.exp(-0.5 * preact * preact)
        below = 1.0 + (0.3275911 * INV_SQRT2) * jnp.abs(preact)
        u = pl.reciprocal(below, approx=True)
        u = u * (2.0 - below * u)
        series = u * (
            0.5 * 0.254829592
            + u * (0.5 * -0.284496736 + u * (0.5 * 1.421413741 + u * (0.5 * -1.453152027 + u * (0.5 * 1.061405429))))
        )
        tail = series * bell
        cdf = jnp.where(preact >= 0.0, 1.0 - tail, tail)
        hidden = (preact * cdf).astype(BF16)
        hid_rows[s] = hidden
        slope = cdf + preact * bell * INV_SQRT_2PI
        branch = dot_last(hidden, w_out[...])
        rows_a[:, 0:C] = branch * scale

        def put_out(t, values):
            total = padded[s, 6 + t, 8:24, :] + values
            block_out[s, :, 128 * t : 128 * t + 128] = (keep_blocks[s, t] * total).astype(BF16)

        from_rows(rows_a, put_out)
        sums[0:1, 0:C] += jnp.sum(seed * branch, axis=0, keepdims=True)
        back_branch = (seed * scale).astype(BF16)
        bb_rows[s] = back_branch
        back_pre = (jnp.dot(back_branch, w_out[...], preferred_element_type=F32) * slope).astype(BF16)
        pre_rows[s] = back_pre
        bias_sums[...] += jnp.sum(back_pre.astype(F32), axis=0, keepdims=True)
        back_shift = dot_last(back_pre, w_in[...])
        sums[1:2, 0:C] += jnp.sum(back_shift * normed, axis=0, keepdims=True)
        sums[2:3, 0:C] += jnp.sum(back_shift, axis=0, keepdims=True)
        scaled = back_shift * gain
        back = inv_std * (
            scaled
            - jnp.mean(scaled, axis=-1, keepdims=True)
            - normed * jnp.mean(scaled * normed, axis=-1, keepdims=True)
        )
        rows_b[:, 0:C] = back.astype(BF16).astype(F32)

        def put_back(t, values):
            blocks[s, t] = values
            back_out[s, :, 128 * t : 128 * t + 128] = values.astype(BF16)

        from_rows(rows_b, put_back)
        return carry

    lax.fori_loop(0, TPD, one_tile, 0, unroll=True)

    emit_strips(lambda s, t, row, rows: blocks[s, t, row : row + rows, :], strip, *strips)
    kernel_grad(padded, shifted_pad, blocks, wide)
    low = low_lanes(TAPS)
    first, middle, last = wide[0, 0:TAPS, :], wide[1, 0:TAPS, :], wide[2, 0:TAPS, :]
    turned_middle, turned_last = pltpu.roll(middle, 64, 1), pltpu.roll(last, 64, 1)
    extra[...] = jnp.zeros_like(extra)
    extra[0:TAPS, :] = first + jnp.where(low, turned_middle, turned_last)
    extra[56 : 56 + TAPS, :] = jnp.where(low, middle + turned_last, 0.0)
    for n in range(3):
        extra[112 + 2 * n : 113 + 2 * n, :] = sums[n : n + 1, 0:128]
        extra[113 + 2 * n : 114 + 2 * n, :] = sums[n : n + 1, 128:256]
    for n in range(6):
        extra[118 + n : 119 + n, :] = bias_sums[0:1, 128 * n : 128 * n + 128]
    grad_in = dot_first(norm_rows[...].reshape(TPD * CELLS, C), pre_rows[...].reshape(TPD * CELLS, HID))
    grad_out = dot_first(bb_rows[...].reshape(TPD * CELLS, C), hid_rows[...].reshape(TPD * CELLS, HID))
    core = lax.rem(lax.axis_index("tiles"), 2)

    def write(target, grad, part, kind):
        for n in range(6):
            target[C * n : C * n + C, :] = grad[:, 128 * n : 128 * n + 128].astype(kind)
        target[6 * C : HALF_ROWS, :] = extra[part * (EXTRA // 2) : (part + 1) * (EXTRA // 2), :].astype(kind)

    @pl.when(core == 0)
    def _():
        write(keep_rows, grad_in, 0, F32)
        write(send_rows, grad_out, 1, BF16)

    @pl.when(core == 1)
    def _():
        write(keep_rows, grad_out, 1, F32)
        write(send_rows, grad_in, 0, BF16)


def field_grad_kernel(tile, *refs):
    back, cotangent, mask, near, dw = refs[0:5]
    given, out = refs[5:13], refs[13]
    padded, shifted_pad, blocks, strip, rows_below, rows_above, right_cols, left_cols, wide, taps = refs[14:]
    for t in range(BLOCKS):
        padded[0, 6 + t, 8:24, :] = back[tile, :, 128 * t : 128 * t + 128].astype(F32)
    spread_taps(dw, wide, taps)
    gather_strips(given, rows_below, rows_above, right_cols, left_cols)
    edges = (rows_below, rows_above, right_cols, left_cols)
    fill_halo(padded, shifted_pad, near, strip, edges, range(tile, tile + 1))
    depthwise(padded, shifted_pad, taps, blocks, True, 1)
    keep = expand_mask(mask, tile)
    for t in range(BLOCKS):
        lanes = slice(128 * t, 128 * t + 128)
        total = cotangent[tile, :, lanes].astype(F32) + blocks[0, t]
        out[0, :, lanes] = (keep[:, lanes] * total).astype(BF16)


def unpack_kernel(rows, grad_kernel, gain, shift, grad_in, bias, grad_out, scale):
    factor = 1.0 / math.sqrt(4 * 64 * TPD * CELLS)

    for n in range(6):
        grad_in[:, 128 * n : 128 * n + 128] = rows[C * n : C * n + C, :].astype(F32) * factor
        at = HALF_ROWS + C * n
        grad_out[:, 128 * n : 128 * n + 128] = rows[at : at + C, :].astype(F32) * factor
    first_part = rows[6 * C : HALF_ROWS, :].astype(F32) * factor
    last_part = rows[HALF_ROWS + 6 * C :, :].astype(F32) * factor
    grad_kernel[:, 0:128] = first_part[0:TAPS, :]
    both = jnp.concatenate([first_part[56:64, :], last_part[0:48, :]], axis=0)
    grad_kernel[:, 128:192] = both[0:TAPS, 0:64]
    tail = last_part[48:64, :]
    for n, target in ((0, scale), (1, gain), (2, shift)):
        target[:, 0:128] = tail[2 * n : 2 * n + 1, :]
        target[:, 128:192] = tail[2 * n + 1 : 2 * n + 2, 0:64]
    for n in range(6):
        bias[128 * n : 128 * n + 128] = tail[6 + n, :]


def whole(memory=pltpu.VMEM):
    return pl.BlockSpec(memory_space=memory)


def call(kernel, inputs, out_shape, scratch, cost, smem=()):
    return pl.pallas_call(
        kernel,
        out_shape=out_shape,
        in_specs=[whole(pltpu.SMEM if n in smem else pltpu.VMEM) for n in range(len(inputs))],
        out_specs=jax.tree.map(lambda _: whole(), out_shape),
        scratch_shapes=scratch,
        compiler_params=pltpu.CompilerParams(vmem_limit_bytes=VMEM_LIMIT),
        cost_estimate=pl.CostEstimate(flops=cost, bytes_accessed=4000000, transcendentals=0),
    )(*inputs)


def halo_scratch():
    return [
        pltpu.VMEM((STRIP, 128), F32),
        pltpu.VMEM((16, STRIP, 128), BF16),
        pltpu.VMEM((16, STRIP, 128), BF16),
        pltpu.VMEM((TPD + 1, STRIP, 128), BF16),
        pltpu.VMEM((TPD + 1, STRIP, 128), BF16),
    ]


def swap(block, axis, partner):
    return lax.ppermute(block, axis, [(i, partner(i)) for i in range(lax.axis_size(axis))])


def first_chip(i):
    return i ^ 2


def second_chip(i):
    j = ((i // 2 + 1) ^ 1) * 2 - 2 + i % 2
    return j if 0 <= j < lax.axis_size("tiles") else i ^ 1


def three_away(i):
    j = i + 3 if i % 2 else i - 3
    return j if 0 <= j < lax.axis_size("tiles") else i ^ 2


def other_core(i):
    return i ^ 1


def relay(early, late, came_early, came_late):
    shape = jax.ShapeDtypeStruct((2 * TPD + 3, STRIP, 128), BF16)
    return call(relay_kernel, (early, late, came_early, came_late), shape, [], 10**5)


def exchange_strips(strips):
    early, late, far, right_own, left_own = strips
    came_far = swap(far, "tiles", three_away)
    came_early = swap(early, "tiles", first_chip)
    came_late = swap(late, "tiles", second_chip)
    came_far, came_early, came_late = lax.optimization_barrier((came_far, came_early, came_late))
    passed = swap(relay(early, late, came_early, came_late), "tiles", other_core)
    return (early, late, right_own, left_own, came_early, came_late, came_far, passed)


MOVES = {"x1": (1, 0), "x2": (3, 0), "y1": (0, 2), "y2": (0, 6), "z1": (0, 8), "z2": (0, 24), "z3": (0, 56)}
ORDERS = (("x1", "x2", "y1", "y2", "z1", "z2", "z3"), ("y1", "y2", "x1", "x2", "z1", "z2", "z3"))


def trade(block, step):
    samples, tiles = lax.axis_size("dp"), lax.axis_size("tiles")
    route = []
    for x in range(samples):
        for t in range(tiles):
            over_x, over_t = MOVES[ORDERS[t % 2][step]]
            route.append((x * tiles + t, (x ^ over_x) * tiles + (t ^ over_t)))
    return lax.ppermute(block, ("dp", "tiles"), route)


def reduce_and_exchange(keep, send, strips, finish):
    early, late, far, right_own, left_own = strips
    barrier = lax.optimization_barrier
    place = lax.axis_index("tiles")
    core, y = place % 2, (place // 2) % 4
    x = lax.axis_index("dp")
    at = {"x1": (x + x // 2) % 2, "x2": x // 2, "y1": (y + y // 2) % 2, "y2": y // 2}
    bits = [jnp.where(core == 0, at[ORDERS[0][n]], at[ORDERS[1][n]]) for n in range(3)]

    def halves(block, bit):
        n = block.shape[0] // 2
        own = lax.dynamic_slice_in_dim(block, bit * n, n, 0)
        return own, lax.dynamic_slice_in_dim(block, (1 - bit) * n, n, 0).astype(BF16)

    def join(block, other, bit):
        return jnp.where(bit == 0, jnp.concatenate([block, other], 0), jnp.concatenate([other, block], 0))

    came_far = swap(far, "tiles", three_away)
    own, other = halves(keep + swap(send, "tiles", other_core).astype(F32), bits[0])
    other, early = barrier((other, early))
    came_early = swap(early, "tiles", first_chip)
    came, came_far = barrier((trade(other, 0), came_far))
    own, other = halves(own + came.astype(F32), bits[1])
    other, late = barrier((other, late))
    came_late = swap(late, "tiles", second_chip)
    came, came_early = barrier((trade(other, 1), came_early))
    own, other = halves(own + came.astype(F32), bits[2])
    came, came_late = barrier((trade(other, 2), came_late))
    mine = own + came.astype(F32)
    between = relay(early, late, came_early, came_late)
    sent, between = barrier((mine.astype(BF16), between))
    passed = swap(between, "tiles", other_core)
    mine = sent.astype(F32) + trade(sent, 3).astype(F32)
    sent = mine.astype(BF16)
    came, passed = barrier((trade(sent, 4), passed))
    mine = sent.astype(F32) + came.astype(F32)
    given = (early, late, right_own, left_own, came_early, came_late, came_far, passed)
    parts = []

    def beside(sent, step):
        nonlocal given
        sent, given = barrier((sent, given))
        came, part = barrier((trade(sent, step), finish(len(parts), given)))
        parts.append(part)
        return sent, came

    for step in (5, 6):
        sent, came = beside(mine.astype(BF16), step)
        mine = sent.astype(F32) + came.astype(F32)
    mine = mine.astype(BF16)
    for step in (2, 1):
        mine, came = beside(mine, step)
        mine = join(mine, came, bits[step])
    mine = join(mine, trade(mine, 0), bits[0])
    return join(mine, swap(mine, "tiles", other_core), core), jnp.concatenate(parts, 0)


def shards(
    fields, ocean_mask, neighbours, dw_kernel, ln_gain, ln_bias, w_in, b_in, w_out, layer_scale, cotangent
):
    tiles = fields.reshape(TPD, TILE, WIDTH)
    cot = cotangent.reshape(TPD, TILE, WIDTH)
    tile_shape = jax.ShapeDtypeStruct((TPD, TILE, WIDTH), BF16)
    block_scratch = pltpu.VMEM((TPD, BLOCKS, TILE, 128), F32)
    pad_scratch = pltpu.VMEM((TPD, PAD_BLOCKS, 32, 128), F32)
    tap_scratch = [pltpu.VMEM((3, 56, 128), F32), pltpu.VMEM((3 * TAPS, 8, 128), F32)]

    strips = call(
        prepare_kernel, (tiles, ocean_mask), strip_shapes(), [block_scratch, pltpu.VMEM((STRIP, 128), F32)], 10**6
    )
    given = exchange_strips(strips)
    row = lambda v: v.reshape(1, -1)
    weights = jnp.concatenate([w_in, w_out.T], 0)
    outs = call(
        block_kernel,
        (
            tiles, cot, ocean_mask, neighbours, dw_kernel, row(ln_gain), row(ln_bias), weights, row(b_in),
            row(layer_scale), *given,
        ),
        [
            tile_shape,
            tile_shape,
            jax.ShapeDtypeStruct((HALF_ROWS, 128), F32),
            jax.ShapeDtypeStruct((HALF_ROWS, 128), BF16),
            *strip_shapes(),
        ],
        [
            pad_scratch, pad_scratch, block_scratch, block_scratch, *halo_scratch(), *tap_scratch,
            pltpu.VMEM((TPD, CELLS, 256), F32),
            pltpu.VMEM((TPD, CELLS, 256), F32),
            pltpu.VMEM((TPD, CELLS, C), BF16),
            pltpu.VMEM((TPD, CELLS, HID), BF16),
            pltpu.VMEM((TPD, CELLS, C), BF16),
            pltpu.VMEM((TPD, CELLS, HID), BF16),
            pltpu.VMEM((8, 256), F32),
            pltpu.VMEM((1, HID), F32),
            pltpu.VMEM((EXTRA, 128), F32),
        ],
        2 * 10**9,
        smem=(3,),
    )
    block_out, back, keep_rows, send_rows = outs[0:4]

    def finish(tile, given):
        return call(
            functools.partial(field_grad_kernel, tile),
            (back, cot, ocean_mask, neighbours, dw_kernel, *given),
            jax.ShapeDtypeStruct((1, TILE, WIDTH), BF16),
            [
                pltpu.VMEM((1, PAD_BLOCKS, 32, 128), F32),
                pltpu.VMEM((1, PAD_BLOCKS, 32, 128), F32),
                pltpu.VMEM((1, BLOCKS, TILE, 128), F32),
                *halo_scratch(),
                *tap_scratch,
            ],
            10**9,
            smem=(3,),
        )

    rows, field_grad = reduce_and_exchange(keep_rows, send_rows, outs[4:], finish)
    grads = call(
        unpack_kernel,
        (rows,),
        [
            jax.ShapeDtypeStruct(shape, F32)
            for shape in ((TAPS, C), (1, C), (1, C), (C, HID), (HID,), (C, HID), (1, C))
        ],
        [],
        10**6,
    )
    grad_kernel, gain, shift, grad_in, bias, grad_out, scale = grads
    return (
        block_out.reshape(fields.shape),
        field_grad.reshape(fields.shape),
        grad_kernel,
        gain.reshape(-1),
        shift.reshape(-1),
        grad_in,
        bias,
        grad_out.T,
        scale.reshape(-1),
    )


def solution(mesh):
    cells = P("dp", "tiles", None, None)
    in_specs = (cells, P("tiles", None, None), P("tiles", None)) + (P(),) * 7 + (cells,)
    out_specs = (cells, cells) + (P(),) * 7
    return jax.shard_map(shards, mesh=mesh, in_specs=in_specs, out_specs=out_specs, check_vma=False)
```

```python
import functools
import math

import jax
import jax.numpy as jnp
from jax import lax
from jax.experimental import pallas as pl
from jax.experimental.pallas import tpu as pltpu
from jax.sharding import PartitionSpec as P

KS = 7
TAPS = KS * KS
TPD = 4
TILE = 16
C = 192
HID = 768
WIDTH = TILE * C
BLOCKS = WIDTH // 128
PAD_BLOCKS = 36
STRIP = 80
CELLS = TILE * TILE
INV_SQRT2 = 0.7071067811865476
LOG_SQRT_2PI = 0.5 * math.log(2.0 * math.pi)
TAIL = [
    0.5 * math.sqrt(2.0 * math.pi) * c
    for c in (0.254829592, -0.284496736, 1.421413741, -1.453152027, 1.061405429)
]
EXTRA = 128
HALF_ROWS = 6 * C + EXTRA // 2
F32 = jnp.float32
BF16 = jnp.bfloat16
VMEM_LIMIT = 20 * 1024 * 1024


def low_lanes(rows):
    return lax.broadcasted_iota(jnp.int32, (rows, 128), 1) < 64


def expand_mask(mask_ref, s):
    cell = lax.broadcasted_iota(jnp.int32, (TILE, WIDTH), 0) * C
    lane = lax.broadcasted_iota(jnp.int32, (TILE, WIDTH), 1)
    spread = jnp.where((lane >= cell) & (lane < cell + C), 1.0, 0.0).astype(BF16)
    keep = (mask_ref[s] > 0).astype(F32).astype(BF16)
    return jnp.dot(keep, spread, preferred_element_type=F32)


def up_comes_first():
    return lax.rem(lax.div(lax.axis_index("tiles"), 2), 2) == 0


def core_is_first():
    return lax.rem(lax.axis_index("tiles"), 2) == 0


def emit_strips(tile_block, strip, early, late, far, right_own, left_own):
    even, first_core = up_comes_first(), core_is_first()
    higher, lower = jnp.where(even, 0, 1), jnp.where(even, 1, 0)

    def put(place, entry, rows, values):
        @pl.when(place == 0)
        def _():
            early[entry, rows, :] = values

        @pl.when(place == 1)
        def _():
            late[entry, rows, :] = values

    everything = slice(0, STRIP)
    strip[72:80, :] = jnp.zeros((8, 128), F32)
    for s in range(TPD):
        for t in range(BLOCKS):
            strip[3 * t : 3 * t + 3, :] = tile_block(s, t, 13, 3)
        top = strip[...].astype(BF16)
        put(higher, s, everything, top)
        for t in range(BLOCKS):
            strip[3 * t : 3 * t + 3, :] = tile_block(s, t, 0, 3)
        bottom = strip[...].astype(BF16)
        put(lower, s, everything, bottom)
        if s == 0:

            @pl.when(first_core)
            def _(bottom=bottom):
                far[0] = bottom

        if s == TPD - 1:

            @pl.when(jnp.logical_not(first_core))
            def _(top=top):
                far[0] = top

        for t in range(5):
            rows = slice(16 * t, 16 * t + 16)
            right = tile_block(s, 19 + t, 0, 16).astype(BF16)
            left = tile_block(s, t, 0, 16).astype(BF16)
            if s == TPD - 1:
                put(higher, TPD, rows, right)
            else:
                right_own[s, rows, :] = right
            if s == 0:
                put(lower, TPD, rows, left)
            else:
                left_own[s - 1, rows, :] = left


def strip_shapes():
    return [jax.ShapeDtypeStruct((n, STRIP, 128), BF16) for n in (TPD + 1, TPD + 1, 1, TPD - 1, TPD - 1)]


def by_chip(early, late, came_early, came_late, work):
    even = up_comes_first()

    @pl.when(even)
    def _():
        work(early, late, came_late, came_early)

    @pl.when(jnp.logical_not(even))
    def _():
        work(late, early, came_early, came_late)


def by_core(first, second):
    is_first = core_is_first()

    @pl.when(is_first)
    def _():
        first()

    @pl.when(jnp.logical_not(is_first))
    def _():
        second()


def relay_kernel(early, late, came_early, came_late, relay):
    def work(own_down, own_up, lower, higher):
        def fill(own, whole, one):
            for n in range(TPD + 1):
                relay[n] = own[n]
                relay[TPD + 1 + n] = whole[n]
            relay[2 * TPD + 2] = one[...]

        by_core(
            lambda: fill(own_down, higher, lower.at[TPD - 1]),
            lambda: fill(own_up, lower, higher.at[0]),
        )

    by_chip(early, late, came_early, came_late, work)


def gather_strips(given, rows_below, rows_above, right_cols, left_cols):
    early, late, right_own, left_own, came_early, came_late, came_far, relay = given
    for s in range(TPD - 1):
        right_cols[1 + s] = right_own[s]
        left_cols[1 + s] = left_own[s]

    def work(own_down, own_up, lower, higher):
        for s in range(TPD):
            rows_below[4 + s] = lower[s]
            rows_below[12 + s] = own_down[s]
            rows_above[s] = own_up[s]
            rows_above[8 + s] = higher[s]
        right_cols[TPD] = own_down[TPD]
        left_cols[0] = own_up[TPD]

    by_chip(early, late, came_early, came_late, work)

    def place(below, above, one_below, one_above):
        rows_below[3] = one_below[...]
        rows_above[12] = one_above[...]
        for s in range(TPD):
            rows_below[8 + s] = relay[below + s]
            rows_above[4 + s] = relay[above + s]
        right_cols[0] = relay[below + TPD]
        left_cols[TPD] = relay[above + TPD]

    last = 2 * TPD + 2
    by_core(
        lambda: place(TPD + 1, 0, came_far.at[0], relay.at[last]),
        lambda: place(0, TPD + 1, relay.at[last], came_far.at[0]),
    )


def fill_halo(padded, shifted, near_ref, strip, edges, tiles):
    rows_below, rows_above, right_cols, left_cols = edges
    first = lax.axis_index("tiles") * TPD

    def one_tile(s, carry):
        tile = tiles[0] + s

        def fetch(direction, source, base, count):
            slot = near_ref[tile, direction]
            place = jnp.clip(slot - first + base, 0, count - 1)
            values = source[place].astype(F32)
            return jnp.where(slot >= 0, values, 0.0)

        def put_rows(values, row, source_block, target_block, count):
            strip[...] = values
            for t in range(count):
                at = 3 * (source_block + t)
                padded[s, target_block + t, row : row + 3, :] = strip[at : at + 3, :]

        put_rows(fetch(1, rows_below, 12, 16), 5, 0, 6, BLOCKS)
        put_rows(fetch(0, rows_below, 12, 16), 5, 19, 1, 5)
        put_rows(fetch(2, rows_below, 12, 16), 5, 0, 30, 5)
        put_rows(fetch(6, rows_above, 0, 16), 24, 0, 6, BLOCKS)
        put_rows(fetch(5, rows_above, 0, 16), 24, 19, 1, 5)
        put_rows(fetch(7, rows_above, 0, 16), 24, 0, 30, 5)
        west = fetch(3, right_cols, 1, TPD + 1)
        east = fetch(4, left_cols, 0, TPD + 1)
        for t in range(5):
            padded[s, 1 + t, 8:24, :] = west[16 * t : 16 * t + 16, :]
            padded[s, 30 + t, 8:24, :] = east[16 * t : 16 * t + 16, :]
        low = low_lanes(32)
        turned = pltpu.roll(padded[s, 1], 64, 1)
        for t in range(1, 34):
            following = pltpu.roll(padded[s, t + 1], 64, 1)
            shifted[s, t] = jnp.where(low, turned, following)
            turned = following
        return carry

    lax.fori_loop(0, len(tiles), one_tile, 0, unroll=True)


def spread_taps(dw_ref, wide, taps):
    low = low_lanes(TAPS)
    first = dw_ref[:, 0:128]
    last = dw_ref[:, 64:192]
    wide[0, 0:TAPS, :] = first
    turned_first = pltpu.roll(first, 64, 1)
    turned_last = pltpu.roll(last, 64, 1)
    wide[1, 0:TAPS, :] = jnp.where(low, turned_last, turned_first)
    wide[2, 0:TAPS, :] = last
    for k in range(TAPS):
        for m in range(3):
            taps[3 * k + m] = jnp.broadcast_to(wide[m, k : k + 1, :], (8, 128))


def windows(padded, shifted, s, m, row):
    half = BLOCKS // 3
    even = [shifted[s, 1 + m + 3 * n, pl.ds(row, 8), :] for n in range(half + 3)]
    odd = [padded[s, 3 + m + 3 * n, pl.ds(row, 8), :] for n in range(half + 2)]
    return lambda q, j: (odd if j % 2 else even)[q + j // 2]


def depthwise(padded, shifted, taps, out, flip, count=TPD):
    half = BLOCKS // 3
    for m in range(3):

        def body(s, carry, m=m):
            for h in range(2):
                total = [None] * half
                for i in range(KS):
                    window = windows(padded, shifted, s, m, 5 + i + 8 * h)
                    for j in range(KS):
                        k = KS * i + j
                        weight = taps[3 * (TAPS - 1 - k if flip else k) + m]
                        for q in range(half):
                            term = window(q, j) * weight
                            total[q] = term if total[q] is None else total[q] + term
                for q in range(half):
                    out[s, 3 * q + m, 8 * h : 8 * h + 8, :] = total[q]
            return carry

        lax.fori_loop(0, count, body, 0, unroll=min(2, count))


def kernel_grad(padded, shifted, back, wide):
    half = BLOCKS // 3
    for m in range(3):
        for i in range(KS):

            def body(s, totals, m=m, i=i):
                totals = list(totals)
                for h in range(2):
                    window = windows(padded, shifted, s, m, 5 + i + 8 * h)
                    here = [back[s, 3 * q + m, 8 * h : 8 * h + 8, :] for q in range(half)]
                    for j in range(KS):
                        for q in range(half):
                            totals[j] = totals[j] + window(q, j) * here[q]
                return tuple(totals)

            start = tuple(jnp.zeros((8, 128), F32) for _ in range(KS))
            totals = lax.fori_loop(0, TPD, body, start, unroll=2)
            for j in range(KS):
                k = KS * i + j
                wide[m, k : k + 1, :] = jnp.sum(totals[j], axis=0, keepdims=True)


def to_rows(block, rows_ref):
    low = low_lanes(TILE)
    for q in range(TILE // 2):
        first, middle, last = block(3 * q), block(3 * q + 1), block(3 * q + 2)
        even = slice(32 * q, 32 * q + 16)
        odd = slice(32 * q + 16, 32 * q + 32)
        rows_ref[even, 0:128] = first
        rows_ref[even, 128:256] = middle
        turned = pltpu.roll(last, 64, 1)
        rows_ref[odd, 0:128] = jnp.where(low, pltpu.roll(middle, 64, 1), turned)
        rows_ref[odd, 128:256] = turned


def from_rows(rows_ref, put):
    low = low_lanes(TILE)
    for q in range(TILE // 2):
        even = slice(32 * q, 32 * q + 16)
        odd = slice(32 * q + 16, 32 * q + 32)
        turned = pltpu.roll(rows_ref[odd, 0:128], 64, 1)
        put(3 * q, rows_ref[even, 0:128])
        put(3 * q + 1, jnp.where(low, rows_ref[even, 128:256], turned))
        put(3 * q + 2, jnp.where(low, turned, pltpu.roll(rows_ref[odd, 128:256], 64, 1)))


def dot_last(left, right):
    return lax.dot_general(left, right, (((1,), (1,)), ((), ())), preferred_element_type=F32)


def dot_first(left, right):
    return lax.dot_general(left, right, (((0,), (0,)), ((), ())), preferred_element_type=F32)


def prepare_kernel(fields, mask, *refs):
    strips, (blocks, strip) = refs[0:5], refs[5:]
    for s in range(TPD):
        keep = expand_mask(mask, s) > 0.5
        values = jnp.where(keep, fields[s].astype(F32), 0.0)
        for t in range(BLOCKS):
            blocks[s, t] = values[:, 128 * t : 128 * t + 128]
    emit_strips(lambda s, t, row, rows: blocks[s, t, row : row + rows, :], strip, *strips)


def block_kernel(*refs):
    fields, cotangent, mask, near, dw, gain_ref, bias_ref, weights, b_in, scale_ref = refs[0:10]
    given = refs[10:18]
    block_out, back_out, keep_rows, send_rows = refs[18:22]
    strips = refs[22:27]
    w_in, w_out = weights.at[0:C], weights.at[C : 2 * C]
    (
        padded, shifted_pad, keep_blocks, blocks, strip, rows_below, rows_above, right_cols, left_cols,
        wide, taps, rows_a_all, rows_b_all, norm_rows, hid_rows, bb_rows, pre_rows, sums, bias_sums, extra,
    ) = refs[27:]

    for s in range(TPD):
        keep = expand_mask(mask, s)
        values = jnp.where(keep > 0.5, fields[s].astype(F32), 0.0)
        for t in range(BLOCKS):
            padded[s, 6 + t, 8:24, :] = values[:, 128 * t : 128 * t + 128]
            keep_blocks[s, t] = keep[:, 128 * t : 128 * t + 128]
    spread_taps(dw, wide, taps)
    gather_strips(given, rows_below, rows_above, right_cols, left_cols)
    edges = (rows_below, rows_above, right_cols, left_cols)
    fill_halo(padded, shifted_pad, near, strip, edges, range(TPD))
    depthwise(padded, shifted_pad, taps, blocks, False)

    sums[...] = jnp.zeros_like(sums)
    bias_sums[...] = jnp.zeros_like(bias_sums)

    def one_tile(s, carry):
        rows_a, rows_b = rows_a_all.at[s], rows_b_all.at[s]
        gain, scale = gain_ref[...], scale_ref[...]
        to_rows(lambda t: blocks[s, t], rows_a)
        to_rows(
            lambda t: cotangent[s, :, 128 * t : 128 * t + 128].astype(F32) * keep_blocks[s, t], rows_b
        )
        conv = rows_a[:, 0:C]
        seed = rows_b[:, 0:C]
        centred = conv - jnp.mean(conv, axis=-1, keepdims=True)
        inv_std = lax.rsqrt(jnp.mean(centred * centred, axis=-1, keepdims=True) + 1e-06)
        normed = centred * inv_std
        shifted = (normed * gain + bias_ref[...]).astype(BF16)
        norm_rows[s] = shifted
        preact = jnp.dot(shifted, w_in[...], preferred_element_type=F32) + b_in[...]
        bell = jnp.exp(-0.5 * preact * preact - LOG_SQRT_2PI)
        below = 1.0 + (0.3275911 * INV_SQRT2) * jnp.abs(preact)
        u = pl.reciprocal(below, approx=True)
        u = u * (2.0 - below * u)
        series = u * (TAIL[0] + u * (TAIL[1] + u * (TAIL[2] + u * (TAIL[3] + u * TAIL[4]))))
        tail = series * bell
        cdf = jnp.where(preact >= 0.0, 1.0 - tail, tail)
        hidden = (preact * cdf).astype(BF16)
        hid_rows[s] = hidden
        slope = cdf + preact * bell
        branch = dot_last(hidden, w_out[...])
        rows_a[:, 0:C] = branch * scale

        def put_out(t, values):
            total = padded[s, 6 + t, 8:24, :] + values
            block_out[s, :, 128 * t : 128 * t + 128] = (keep_blocks[s, t] * total).astype(BF16)

        from_rows(rows_a, put_out)
        sums[0:1, 0:C] += jnp.sum(seed * branch, axis=0, keepdims=True)
        back_branch = (seed * scale).astype(BF16)
        bb_rows[s] = back_branch
        back_pre = (jnp.dot(back_branch, w_out[...], preferred_element_type=F32) * slope).astype(BF16)
        pre_rows[s] = back_pre
        bias_sums[...] += jnp.sum(back_pre.astype(F32), axis=0, keepdims=True)
        back_shift = dot_last(back_pre, w_in[...])
        sums[1:2, 0:C] += jnp.sum(back_shift * normed, axis=0, keepdims=True)
        sums[2:3, 0:C] += jnp.sum(back_shift, axis=0, keepdims=True)
        scaled = back_shift * gain
        back = inv_std * (
            scaled
            - jnp.mean(scaled, axis=-1, keepdims=True)
            - normed * jnp.mean(scaled * normed, axis=-1, keepdims=True)
        )
        rows_b[:, 0:C] = back.astype(BF16).astype(F32)

        def put_back(t, values):
            blocks[s, t] = values
            back_out[s, :, 128 * t : 128 * t + 128] = values.astype(BF16)

        from_rows(rows_b, put_back)
        return carry

    lax.fori_loop(0, TPD, one_tile, 0, unroll=True)

    emit_strips(lambda s, t, row, rows: blocks[s, t, row : row + rows, :], strip, *strips)
    kernel_grad(padded, shifted_pad, blocks, wide)
    low = low_lanes(TAPS)
    first, middle, last = wide[0, 0:TAPS, :], wide[1, 0:TAPS, :], wide[2, 0:TAPS, :]
    turned_middle, turned_last = pltpu.roll(middle, 64, 1), pltpu.roll(last, 64, 1)
    extra[...] = jnp.zeros_like(extra)
    extra[0:TAPS, :] = first + jnp.where(low, turned_middle, turned_last)
    extra[56 : 56 + TAPS, :] = jnp.where(low, middle + turned_last, 0.0)
    for n in range(3):
        extra[112 + 2 * n : 113 + 2 * n, :] = sums[n : n + 1, 0:128]
        extra[113 + 2 * n : 114 + 2 * n, :] = sums[n : n + 1, 128:256]
    for n in range(6):
        extra[118 + n : 119 + n, :] = bias_sums[0:1, 128 * n : 128 * n + 128]
    grad_in = dot_first(norm_rows[...].reshape(TPD * CELLS, C), pre_rows[...].reshape(TPD * CELLS, HID))
    grad_out = dot_first(bb_rows[...].reshape(TPD * CELLS, C), hid_rows[...].reshape(TPD * CELLS, HID))
    core = lax.rem(lax.axis_index("tiles"), 2)

    def write(target, grad, part, kind):
        for n in range(6):
            target[C * n : C * n + C, :] = grad[:, 128 * n : 128 * n + 128].astype(kind)
        target[6 * C : HALF_ROWS, :] = extra[part * (EXTRA // 2) : (part + 1) * (EXTRA // 2), :].astype(kind)

    @pl.when(core == 0)
    def _():
        write(keep_rows, grad_in, 0, F32)
        write(send_rows, grad_out, 1, BF16)

    @pl.when(core == 1)
    def _():
        write(keep_rows, grad_out, 1, F32)
        write(send_rows, grad_in, 0, BF16)


def field_grad_kernel(tile, *refs):
    back, cotangent, mask, near, dw = refs[0:5]
    given, out = refs[5:13], refs[13]
    padded, shifted_pad, blocks, strip, rows_below, rows_above, right_cols, left_cols, wide, taps = refs[14:]
    for t in range(BLOCKS):
        padded[0, 6 + t, 8:24, :] = back[tile, :, 128 * t : 128 * t + 128].astype(F32)
    spread_taps(dw, wide, taps)
    gather_strips(given, rows_below, rows_above, right_cols, left_cols)
    edges = (rows_below, rows_above, right_cols, left_cols)
    fill_halo(padded, shifted_pad, near, strip, edges, range(tile, tile + 1))
    depthwise(padded, shifted_pad, taps, blocks, True, 1)
    keep = expand_mask(mask, tile)
    for t in range(BLOCKS):
        lanes = slice(128 * t, 128 * t + 128)
        total = cotangent[tile, :, lanes].astype(F32) + blocks[0, t]
        out[0, :, lanes] = (keep[:, lanes] * total).astype(BF16)


def unpack_kernel(rows, grad_kernel, gain, shift, grad_in, bias, grad_out, scale):
    factor = 1.0 / math.sqrt(4 * 64 * TPD * CELLS)

    for n in range(6):
        grad_in[:, 128 * n : 128 * n + 128] = rows[C * n : C * n + C, :].astype(F32) * factor
        at = HALF_ROWS + C * n
        grad_out[:, 128 * n : 128 * n + 128] = rows[at : at + C, :].astype(F32) * factor
    first_part = rows[6 * C : HALF_ROWS, :].astype(F32) * factor
    last_part = rows[HALF_ROWS + 6 * C :, :].astype(F32) * factor
    grad_kernel[:, 0:128] = first_part[0:TAPS, :]
    both = jnp.concatenate([first_part[56:64, :], last_part[0:48, :]], axis=0)
    grad_kernel[:, 128:192] = both[0:TAPS, 0:64]
    tail = last_part[48:64, :]
    for n, target in ((0, scale), (1, gain), (2, shift)):
        target[:, 0:128] = tail[2 * n : 2 * n + 1, :]
        target[:, 128:192] = tail[2 * n + 1 : 2 * n + 2, 0:64]
    for n in range(6):
        bias[128 * n : 128 * n + 128] = tail[6 + n, :]


def whole(memory=pltpu.VMEM):
    return pl.BlockSpec(memory_space=memory)


def call(kernel, inputs, out_shape, scratch, cost, smem=()):
    return pl.pallas_call(
        kernel,
        out_shape=out_shape,
        in_specs=[whole(pltpu.SMEM if n in smem else pltpu.VMEM) for n in range(len(inputs))],
        out_specs=jax.tree.map(lambda _: whole(), out_shape),
        scratch_shapes=scratch,
        compiler_params=pltpu.CompilerParams(vmem_limit_bytes=VMEM_LIMIT),
        cost_estimate=pl.CostEstimate(flops=cost, bytes_accessed=4000000, transcendentals=0),
    )(*inputs)


def halo_scratch():
    return [
        pltpu.VMEM((STRIP, 128), F32),
        pltpu.VMEM((16, STRIP, 128), BF16),
        pltpu.VMEM((16, STRIP, 128), BF16),
        pltpu.VMEM((TPD + 1, STRIP, 128), BF16),
        pltpu.VMEM((TPD + 1, STRIP, 128), BF16),
    ]


def swap(block, axis, partner):
    return lax.ppermute(block, axis, [(i, partner(i)) for i in range(lax.axis_size(axis))])


def first_chip(i):
    return i ^ 2


def second_chip(i):
    j = ((i // 2 + 1) ^ 1) * 2 - 2 + i % 2
    return j if 0 <= j < lax.axis_size("tiles") else i ^ 1


def three_away(i):
    j = i + 3 if i % 2 else i - 3
    return j if 0 <= j < lax.axis_size("tiles") else i ^ 2


def other_core(i):
    return i ^ 1


def relay(early, late, came_early, came_late):
    shape = jax.ShapeDtypeStruct((2 * TPD + 3, STRIP, 128), BF16)
    return call(relay_kernel, (early, late, came_early, came_late), shape, [], 10**5)


def exchange_strips(strips):
    early, late, far, right_own, left_own = strips
    came_far = swap(far, "tiles", three_away)
    came_early = swap(early, "tiles", first_chip)
    came_late = swap(late, "tiles", second_chip)
    came_far, came_early, came_late = lax.optimization_barrier((came_far, came_early, came_late))
    passed = swap(relay(early, late, came_early, came_late), "tiles", other_core)
    return (early, late, right_own, left_own, came_early, came_late, came_far, passed)


MOVES = {"x1": (1, 0), "x2": (3, 0), "y1": (0, 2), "y2": (0, 6), "z1": (0, 8), "z2": (0, 24), "z3": (0, 56)}
ORDERS = (("x1", "x2", "y1", "y2", "z1", "z2", "z3"), ("y1", "y2", "x1", "x2", "z1", "z2", "z3"))


def trade(block, step):
    samples, tiles = lax.axis_size("dp"), lax.axis_size("tiles")
    route = []
    for x in range(samples):
        for t in range(tiles):
            over_x, over_t = MOVES[ORDERS[t % 2][step]]
            route.append((x * tiles + t, (x ^ over_x) * tiles + (t ^ over_t)))
    return lax.ppermute(block, ("dp", "tiles"), route)


def reduce_and_exchange(keep, send, strips, finish):
    early, late, far, right_own, left_own = strips
    barrier = lax.optimization_barrier
    place = lax.axis_index("tiles")
    core, y = place % 2, (place // 2) % 4
    x = lax.axis_index("dp")
    at = {"x1": (x + x // 2) % 2, "x2": x // 2, "y1": (y + y // 2) % 2, "y2": y // 2}
    bits = [jnp.where(core == 0, at[ORDERS[0][n]], at[ORDERS[1][n]]) for n in range(3)]

    def halves(block, bit):
        n = block.shape[0] // 2
        own = lax.dynamic_slice_in_dim(block, bit * n, n, 0)
        return own, lax.dynamic_slice_in_dim(block, (1 - bit) * n, n, 0).astype(BF16)

    def join(block, other, bit):
        return jnp.where(bit == 0, jnp.concatenate([block, other], 0), jnp.concatenate([other, block], 0))

    came_far = swap(far, "tiles", three_away)
    own, other = halves(keep + swap(send, "tiles", other_core).astype(F32), bits[0])
    other, early = barrier((other, early))
    came_early = swap(early, "tiles", first_chip)
    came, came_far = barrier((trade(other, 0), came_far))
    own, other = halves(own + came.astype(F32), bits[1])
    other, late = barrier((other, late))
    came_late = swap(late, "tiles", second_chip)
    came, came_early = barrier((trade(other, 1), came_early))
    own, other = halves(own + came.astype(F32), bits[2])
    came, came_late = barrier((trade(other, 2), came_late))
    mine = own + came.astype(F32)
    between = relay(early, late, came_early, came_late)
    sent, between = barrier((mine.astype(BF16), between))
    passed = swap(between, "tiles", other_core)
    mine = sent.astype(F32) + trade(sent, 3).astype(F32)
    sent = mine.astype(BF16)
    came, passed = barrier((trade(sent, 4), passed))
    mine = sent.astype(F32) + came.astype(F32)
    given = (early, late, right_own, left_own, came_early, came_late, came_far, passed)
    parts = []

    def beside(sent, step):
        nonlocal given
        sent, given = barrier((sent, given))
        came, part = barrier((trade(sent, step), finish(len(parts), given)))
        parts.append(part)
        return sent, came

    for step in (5, 6):
        sent, came = beside(mine.astype(BF16), step)
        mine = sent.astype(F32) + came.astype(F32)
    mine = mine.astype(BF16)
    for step in (2, 1):
        mine, came = beside(mine, step)
        mine = join(mine, came, bits[step])
    mine = join(mine, trade(mine, 0), bits[0])
    return join(mine, swap(mine, "tiles", other_core), core), jnp.concatenate(parts, 0)


def shards(
    fields, ocean_mask, neighbours, dw_kernel, ln_gain, ln_bias, w_in, b_in, w_out, layer_scale, cotangent
):
    tiles = fields.reshape(TPD, TILE, WIDTH)
    cot = cotangent.reshape(TPD, TILE, WIDTH)
    tile_shape = jax.ShapeDtypeStruct((TPD, TILE, WIDTH), BF16)
    block_scratch = pltpu.VMEM((TPD, BLOCKS, TILE, 128), F32)
    pad_scratch = pltpu.VMEM((TPD, PAD_BLOCKS, 32, 128), F32)
    tap_scratch = [pltpu.VMEM((3, 56, 128), F32), pltpu.VMEM((3 * TAPS, 8, 128), F32)]

    strips = call(
        prepare_kernel, (tiles, ocean_mask), strip_shapes(), [block_scratch, pltpu.VMEM((STRIP, 128), F32)], 10**6
    )
    given = exchange_strips(strips)
    row = lambda v: v.reshape(1, -1)
    weights = jnp.concatenate([w_in, w_out.T], 0)
    outs = call(
        block_kernel,
        (
            tiles, cot, ocean_mask, neighbours, dw_kernel, row(ln_gain), row(ln_bias), weights, row(b_in),
            row(layer_scale), *given,
        ),
        [
            tile_shape,
            tile_shape,
            jax.ShapeDtypeStruct((HALF_ROWS, 128), F32),
            jax.ShapeDtypeStruct((HALF_ROWS, 128), BF16),
            *strip_shapes(),
        ],
        [
            pad_scratch, pad_scratch, block_scratch, block_scratch, *halo_scratch(), *tap_scratch,
            pltpu.VMEM((TPD, CELLS, 256), F32),
            pltpu.VMEM((TPD, CELLS, 256), F32),
            pltpu.VMEM((TPD, CELLS, C), BF16),
            pltpu.VMEM((TPD, CELLS, HID), BF16),
            pltpu.VMEM((TPD, CELLS, C), BF16),
            pltpu.VMEM((TPD, CELLS, HID), BF16),
            pltpu.VMEM((8, 256), F32),
            pltpu.VMEM((1, HID), F32),
            pltpu.VMEM((EXTRA, 128), F32),
        ],
        2 * 10**9,
        smem=(3,),
    )
    block_out, back, keep_rows, send_rows = outs[0:4]

    def finish(tile, given):
        return call(
            functools.partial(field_grad_kernel, tile),
            (back, cot, ocean_mask, neighbours, dw_kernel, *given),
            jax.ShapeDtypeStruct((1, TILE, WIDTH), BF16),
            [
                pltpu.VMEM((1, PAD_BLOCKS, 32, 128), F32),
                pltpu.VMEM((1, PAD_BLOCKS, 32, 128), F32),
                pltpu.VMEM((1, BLOCKS, TILE, 128), F32),
                *halo_scratch(),
                *tap_scratch,
            ],
            10**9,
            smem=(3,),
        )

    rows, field_grad = reduce_and_exchange(keep_rows, send_rows, outs[4:], finish)
    grads = call(
        unpack_kernel,
        (rows,),
        [
            jax.ShapeDtypeStruct(shape, F32)
            for shape in ((TAPS, C), (1, C), (1, C), (C, HID), (HID,), (C, HID), (1, C))
        ],
        [],
        10**6,
    )
    grad_kernel, gain, shift, grad_in, bias, grad_out, scale = grads
    return (
        block_out.reshape(fields.shape),
        field_grad.reshape(fields.shape),
        grad_kernel,
        gain.reshape(-1),
        shift.reshape(-1),
        grad_in,
        bias,
        grad_out.T,
        scale.reshape(-1),
    )


def solution(mesh):
    cells = P("dp", "tiles", None, None)
    in_specs = (cells, P("tiles", None, None), P("tiles", None)) + (P(),) * 7 + (cells,)
    out_specs = (cells, cells) + (P(),) * 7
    return jax.shard_map(shards, mesh=mesh, in_specs=in_specs, out_specs=out_specs, check_vma=False)
```
